32 devices in a mesh: rep: 2 (over y), span: 2 (over x), seq: 4 (over z), head: 2 (over core).
Axes of the slice: x: 2, y: 2, z: 4, core: 2. Of those that a mesh axis runs over, the one named last changes fastest.
Arguments:
- queries: bfloat16 [4, 2, 1024, 4096], P(('rep', 'span'), 'head', None, 'seq'), parts along dimension 0, may hold values from -12 to 12
- keys: bfloat16 [4, 2, 1024, 4096], P(('rep', 'span'), 'head', None, 'seq'), parts along dimension 0, may hold values from -12 to 12
- values: bfloat16 [4, 2, 1024, 4096], P(('rep', 'span'), 'head', None, 'seq'), parts along dimension 0, may hold values from -6 to 6
- span_order: int32 [4], P('rep'), parts along dimension 0, may hold values from 0 to 15, as said below
Outputs:
- attention: bfloat16 [4, 2, 1024, 4096], P(('rep', 'span'), 'head', 'seq'), parts along dimension 0
The draws below stay inside these ranges and needn't reach their ends.
There are 2 independent parts, one for each index of `rep`. The reference program is written for one: setup_inputs(seed, part) draws one part's arguments, and reference() takes and returns one part's arrays. A program takes and returns all parts, laid end to end along the dimension named above; each array names one. Nothing has to cross between parts.
Inputs may be any that keep to these rules, and one draw needn't show every extreme that they name: `span_order`: each group has a different span index.
All inputs are finite; a program needn't handle non-finite values.
Results may differ from the reference program's by a relative error of at most 0.0055.
Values may be sent and summed in bfloat16 or wider, within the bound.
No kernel may reach another device: no remote copies, remote signals or barrier semaphores. Data moves between devices by JAX's collectives and lax.ppermute only.
A program may use at most 128 MiB of HBM per device.

```python
import math
import jax
import jax.numpy as jnp
from jax import lax

HD = 128
HALF = 1024
GROUPS = 2
EMBED = 4096
N_HEAD = 2


def pair_draw(key):
    full_shape = (GROUPS, N_HEAD, HALF, EMBED)
    query_key = jax.random.fold_in(key, 11)
    key_key = jax.random.fold_in(key, 12)
    queries = jnp.clip(2.5 * jax.random.normal(query_key, full_shape, jnp.float32), -10.0, 10.0)
    keys = jnp.clip(jax.random.normal(key_key, full_shape, jnp.float32), -4.0, 4.0)
    return (queries, keys)


def draw_queries(key, part):
    return pair_draw(key)[0].astype(jnp.bfloat16)


def draw_keys(key, part):
    return pair_draw(key)[1].astype(jnp.bfloat16)


def draw_span_order(key, part):
    order_key = jax.random.fold_in(key, 21)
    shuffled = jax.random.permutation(order_key, jnp.arange(8 * GROUPS, dtype=jnp.int32))
    return shuffled[:GROUPS].astype(jnp.int32)


def level_of(rng, shape, pieces, smallest, largest):
    factor_of, own = 1.0, jax.random.fold_in(rng, 6)
    for position, shards_of in pieces:
        steps = jnp.exp(jax.random.uniform(jax.random.fold_in(own, position), (shards_of,), jnp.float32, smallest / len(pieces), largest / len(pieces)))
        factor_of = factor_of * jnp.repeat(steps, shape[position] // shards_of).reshape([-1 if axis == position else 1 for axis in range(len(shape))])
    return factor_of


def noise(own_key, shape, deviation, most, pieces=(), held_as=jnp.bfloat16):
    factor_of = level_of(own_key, shape, pieces, -0.22, 0.18) if pieces else 1.0
    entries = jax.random.normal(own_key, shape, jnp.float32) * deviation * factor_of
    return jnp.minimum(jnp.maximum(entries, -most), most).astype(held_as)


def setup_inputs(seed: int = 0, part: int = 0) -> dict:
    splits = jax.random.split(jax.random.key(seed), 5)
    own_keys = jax.random.split(jax.random.fold_in(splits[4], part), 5)
    queries = draw_queries(jax.random.fold_in(jax.random.fold_in(splits[4], part), 71), part)
    keys = draw_keys(jax.random.fold_in(jax.random.fold_in(splits[4], part), 71), part)
    values = noise(own_keys[2], (GROUPS, N_HEAD, HALF, EMBED), 1.0, 6.0, ((0, 2), (1, 2), (3, 4)))
    span_order = draw_span_order(jax.random.fold_in(jax.random.fold_in(splits[4], part), 71), part)
    return {"queries": queries, "keys": keys, "values": values, "span_order": span_order}


def reference(queries, keys, values, span_order):
    group_count = queries.shape[0]
    span_len = queries.shape[1] * queries.shape[2]
    embed_width = queries.shape[3]
    head_count = embed_width // HD
    score_scale = 1.0 / math.sqrt(HD)
    bias_rate = 1.0 / (2.0 * group_count)
    key_heads = keys.reshape(group_count * span_len, head_count, HD).transpose(1, 0, 2)
    value_heads = values.reshape(group_count * span_len, head_count, HD).transpose(1, 0, 2)
    key_spans = jnp.repeat(span_order, span_len)
    results = []
    for group in range(group_count):
        allowed = key_spans <= span_order[group]
        distance_bias = (span_order[group] - key_spans).astype(jnp.float32) * jnp.float32(bias_rate)

        def one_head(inputs):
            query_head, key_head, value_head = inputs
            scores = jnp.dot(query_head.astype(jnp.float32), key_head.astype(jnp.float32).T) * score_scale
            scores = scores - distance_bias[None, :]
            scores = jnp.where(allowed[None, :], scores, jnp.float32(-1e+30))
            row_max = lax.optimization_barrier(jnp.max(scores, axis=1, keepdims=True))
            weights = jnp.where(allowed[None, :], jnp.exp(scores - row_max), 0.0).astype(jnp.bfloat16)
            totals = lax.optimization_barrier(jnp.sum(weights.astype(jnp.float32), axis=1, keepdims=True))
            weighted = jnp.dot(weights.astype(jnp.float32), value_head.astype(jnp.float32))
            return (weighted / totals).astype(jnp.bfloat16)
        query_heads = queries[group].reshape(span_len, head_count, HD).transpose(1, 0, 2)
        result = lax.map(one_head, (query_heads, key_heads, value_heads))
        results.append(result.transpose(1, 0, 2).reshape(queries.shape[1], queries.shape[2], embed_width))
    return jnp.stack(results)
```

```python
import functools
import math

import jax
import jax.numpy as jnp
from jax import lax
from jax.experimental import pallas as pl
from jax.experimental.pallas import tpu as pltpu
from jax.sharding import PartitionSpec as P

HD = 128
LOG2E = math.log2(math.e)
SCALE2 = LOG2E / math.sqrt(HD)
ROWS = 512
VMEM = 40 * 2**20
ANY = pl.BlockSpec(memory_space=pl.ANY)
SMEM = pl.BlockSpec(memory_space=pltpu.SMEM)


def lookup(span_order, block_index):
    table = jnp.arange(span_order.shape[0], dtype=jnp.int32)
    return jnp.sum(
        jnp.where(block_index[:, None] == table[None, :], span_order[None, :], 0), axis=1
    )


def initial(query_heads):
    query_count = query_heads.shape[0]
    local_heads = query_heads.shape[1]
    return (
        jnp.full((local_heads, query_count), -1e30, jnp.float32),
        jnp.zeros((local_heads, query_count), jnp.float32),
        jnp.zeros((local_heads, query_count, HD), jnp.float32),
    )


def attend(running, query_heads, key_piece, value_piece, block_span, own_span, bias_rate):
    block_count = key_piece.shape[0]
    piece_rows = key_piece.shape[1]
    local_heads = key_piece.shape[2] // HD
    key_count = block_count * piece_rows
    score_scale = 1.0 / math.sqrt(HD)
    key_spans = jnp.repeat(block_span, piece_rows)
    allowed = key_spans <= own_span
    distance_bias = (own_span - key_spans).astype(jnp.float32) * jnp.float32(bias_rate)
    block_size = 1024
    block_total = key_count // block_size
    key_blocks = key_piece.reshape(block_total, block_size, local_heads, HD)
    value_blocks = value_piece.reshape(block_total, block_size, local_heads, HD)
    allow_blocks = allowed.reshape(block_total, block_size)
    bias_blocks = distance_bias.reshape(block_total, block_size)

    def advance(status, block_item):
        key_block, value_block, allow_block, bias_block = block_item
        maxima, totals, weighted = status
        scores = (
            jnp.einsum("qhd,khd->hqk", query_heads, key_block, preferred_element_type=jnp.float32)
            * score_scale
        )
        scores = scores - bias_block[None, None, :]
        scores = jnp.where(allow_block[None, None, :], scores, jnp.float32(-1e30))
        new_max = jnp.maximum(maxima, jnp.max(scores, axis=2))
        weights = jnp.where(
            allow_block[None, None, :], jnp.exp(scores - new_max[:, :, None]), 0.0
        ).astype(jnp.bfloat16)
        shrink = jnp.exp(maxima - new_max)
        totals = totals * shrink + jnp.sum(weights.astype(jnp.float32), axis=2)
        weighted = weighted * shrink[:, :, None] + jnp.einsum(
            "hqk,khd->hqd", weights, value_block, preferred_element_type=jnp.float32
        )
        return ((new_max, totals, weighted), None)

    running, unused = lax.scan(
        advance, running, (key_blocks, value_blocks, allow_blocks, bias_blocks)
    )
    return running


def finish(running):
    maxima, totals, weighted = running
    local_heads = weighted.shape[0]
    query_count = weighted.shape[1]
    output = (weighted / totals[:, :, None]).transpose(1, 0, 2)
    return output.reshape(1, 1, query_count, local_heads * HD).astype(jnp.bfloat16)


def gathered(queries, keys, values, span_order):
    half_rows = queries.shape[2]
    local_width = queries.shape[3]
    local_heads = local_width // HD
    halves = lax.axis_size("head")
    bias_rate = 1.0 / (2.0 * span_order.shape[0])
    own_span = lookup(span_order, jnp.reshape(lax.axis_index("span"), (1,)))[0]
    query_heads = queries.reshape(half_rows, local_heads, HD)
    pieces = (
        lax.all_gather(keys, ("span", "head"), axis=0, tiled=True),
        lax.all_gather(values, ("span", "head"), axis=0, tiled=True),
    )
    count = pieces[0].shape[0]
    block_index = jnp.arange(count, dtype=jnp.int32) // halves
    key_piece = pieces[0].reshape(count, half_rows, local_width)
    value_piece = pieces[1].reshape(count, half_rows, local_width)
    running = attend(
        initial(query_heads),
        query_heads,
        key_piece,
        value_piece,
        lookup(span_order, block_index),
        own_span,
        bias_rate,
    )
    result = finish(running)
    return lax.all_to_all(result, "seq", split_axis=2, concat_axis=3, tiled=True)


def rows_by_cols(a, b):
    return lax.dot_general(a, b, (((1,), (1,)), ((), ())), preferred_element_type=jnp.float32)


def attend_rows(q, k0, k1, v0, v1):
    parts = []
    for k, v in ((k0, v0), (k1, v1)):
        scores = rows_by_cols(q, k[...])
        top = jnp.max(scores, axis=1, keepdims=True) * SCALE2
        weights = jnp.exp2(scores * SCALE2 - top).astype(jnp.bfloat16)
        parts.append((jnp.dot(weights, v[...], preferred_element_type=jnp.float32), top))
    (a0, m0), (a1, m1) = parts
    top = jnp.maximum(m0, m1)
    both = a0 * jnp.exp2(m0 - top) + a1 * jnp.exp2(m1 - top)
    return both[:, :HD], both[:, HD:], top


def load_values(v0, v1, e0, e1):
    for v, e in ((v0, e0), (v1, e1)):
        e[:, :HD] = v[...]
        e[:, HD:] = jnp.ones_like(e[:, HD:])


def attend_own(q, k0, k1, e0, e1, own, lse):
    for r in range(0, q.shape[0], ROWS):
        block = pl.ds(r, ROWS)
        o, l, m = attend_rows(q[block, :], k0, k1, e0, e1)
        own[block, :] = o / l
        lse[block, :] = m + jnp.log2(l)


def put_pieces(me, own, pieces):
    count = len(pieces)
    size = pieces[0].shape[0]
    for d, piece in enumerate(pieces):
        start = pl.multiple_of(lax.rem(me + d, count) * size, size)
        piece[...] = own[pl.ds(start, size), :].astype(jnp.bfloat16)


def own_kernel(pieces, ints, q, k0, k1, v0, v1, own, lse, *rest):
    out, (e0, e1) = rest[:pieces], rest[pieces:]
    load_values(v0, v1, e0, e1)
    attend_own(q, k0, k1, e0, e1, own, lse)
    put_pieces(ints[1], own, out)


def step_kernel(pieces, ints, xq, q, k0, k1, v0, v1, nq, send, send_lse, own, lse, *rest):
    out, (e0, e1) = rest[:pieces], rest[pieces:]
    part = pl.program_id(0)
    high = ints[0] == 1

    @pl.when(part == 0)
    def _():
        load_values(v0, v1, e0, e1)

    @pl.when((part == 0) & high)
    def _():
        send[...] = nq[...]

    @pl.when((part == 0) & jnp.logical_not(high))
    def _():
        for r in range(0, xq.shape[0], ROWS):
            o, l, m = attend_rows(xq[pl.ds(r, ROWS), :], k0, k1, e0, e1)
            send[pl.ds(r, ROWS), :] = (o / l).astype(jnp.bfloat16)
            level = m + jnp.log2(l)
            for c in range(0, ROWS, HD):
                send_lse[pl.ds((r + c) // HD, 1), :] = level[c : c + HD, :].T[:1, :]

    @pl.when(part == 1)
    def _():
        attend_own(q, k0, k1, e0, e1, own, lse)
        put_pieces(ints[1], own, out)


def blend(o0, l0, o1, l1):
    top = jnp.maximum(l0, l1)
    w0, w1 = jnp.exp2(l0 - top), jnp.exp2(l1 - top)
    return (o0 * w0 + o1 * w1) / (w0 + w1)


def copy_in(pairs, sems):
    copies = [pltpu.make_async_copy(s, d, sems.at[i]) for i, (s, d) in enumerate(pairs)]
    for c in copies:
        c.start()
    for c in copies:
        c.wait()


def merge_kernel(pieces, ints, shift, own, lse, r, rl, *rest):
    out, rest = rest[pieces : 2 * pieces], rest[2 * pieces :]
    own_v, lse_v, r_v, rl_v, out_v, sems = rest

    @pl.when(ints[0] == 1)
    def _():
        copy_in([(own, own_v), (lse, lse_v), (r, r_v), (rl, rl_v)], sems)
        for i in range(0, own_v.shape[0], HD):
            rows = pl.ds(i, HD)
            level = jnp.broadcast_to(rl_v[pl.ds(i // HD, 1), :], (HD, HD)).T - shift[0]
            own_v[rows, :] = blend(own_v[rows, :], lse_v[rows, :], r_v[rows, :].astype(jnp.float32), level)
        put_pieces(ints[1], own_v, [out_v.at[d] for d in range(pieces)])
        copy_in([(out_v.at[d], out[d]) for d in range(pieces)], sems)


def far_kernel(pieces, head, ints, shift, own, lse, q, k0, k1, v0, v1, *rest):
    out, rest = rest[pieces : 2 * pieces], rest[2 * pieces :]
    own_v, lse_v, q_v, k0_v, k1_v, v0_v, v1_v, e0, e1, out_v, sems = rest

    @pl.when(ints[0] == 1)
    def _():
        copy_in(
            [
                (own, own_v), (lse, lse_v), (q.at[:, pl.ds(head * HD, HD)], q_v),
                (k0, k0_v), (k1, k1_v), (v0, v0_v), (v1, v1_v),
            ],
            sems,
        )
        load_values(v0_v, v1_v, e0, e1)
        for i in range(0, own_v.shape[0], ROWS):
            rows = pl.ds(i, ROWS)
            o, l, m = attend_rows(q_v[rows, :], k0_v, k1_v, e0, e1)
            level = m + jnp.log2(l) - shift[0]
            own_v[rows, :] = blend(own_v[rows, :], lse_v[rows, :], o / l, level)
        put_pieces(ints[1], own_v, [out_v.at[d] for d in range(pieces)])
        copy_in([(out_v.at[d], out[d]) for d in range(pieces)], sems)


def place_kernel(heads, pieces, total, first, ints, *rest):
    parts, rest = rest[: len(heads) * pieces], rest[len(heads) * pieces :]
    out, sems = rest[-2:]
    pairs = []
    for a, h in enumerate(heads):
        for d in range(pieces):
            source = lax.rem(ints[1] + (pieces - d), pieces)
            column = pl.multiple_of((source * total + h) * HD, HD)
            pairs.append((parts[a * pieces + d], out.at[:, pl.ds(column, HD)]))
    copy_in(pairs, sems)


def column(index):
    return lambda *_: (0, index)


def fixed(*_):
    return (0, 0)


def cost(units, size):
    return pl.CostEstimate(flops=int(units * 3e9), bytes_accessed=size, transcendentals=0)


def staggered(queries, keys, values, span_order):
    q, k, v = queries[0, 0], keys[0, 0], values[0, 0]
    tokens, width = q.shape
    heads = width // HD
    ring = lax.axis_size("seq")
    piece_rows = tokens // ring
    me = lax.axis_index("seq")
    mine = lax.axis_index("span")
    own_order = lookup(span_order, jnp.reshape(mine, (1,)))[0]
    far_order = lookup(span_order, jnp.reshape(1 - mine, (1,)))[0]
    high = own_order > far_order
    ints = jnp.stack([high.astype(jnp.int32), me.astype(jnp.int32)])
    bias_rate = 1.0 / (2.0 * span_order.shape[0])
    shift = jnp.reshape((own_order - far_order).astype(jnp.float32) * jnp.float32(bias_rate * LOG2E), (1,))
    swap = [(0, 1), (1, 0)]

    def cut(a, h, n=1):
        return a[:, h * HD : (h + n) * HD]

    far_heads = [heads - 1, heads - 2]
    near_heads = list(range(heads - 2))
    lag = 2 * len(far_heads)

    first = []
    for i, (a, h) in enumerate((a, h) for h in far_heads for a in (k, v)):
        first.append(lax.ppermute(jnp.where(high, cut(q, i), cut(a, h)), "span", swap))

    other = {}
    for start, count in ((heads - 1, 1), (heads - 2, 1), (0, 2), (2, heads - 4)):
        kk = lax.ppermute(cut(k, start, count), "head", swap)
        vv = lax.ppermute(cut(v, start, count), "head", swap)
        for j in range(count):
            other[start + j] = (kk, vv, j)

    head_block = (tokens, HD)
    full = pl.BlockSpec(head_block, fixed)
    piece = pl.BlockSpec((piece_rows, HD), fixed)
    wide = jax.ShapeDtypeStruct(head_block, jnp.float32)
    thin = jax.ShapeDtypeStruct(head_block, jnp.bfloat16)
    levels = jax.ShapeDtypeStruct((tokens // HD, HD), jnp.float32)
    small = jax.ShapeDtypeStruct((piece_rows, HD), jnp.bfloat16)
    extended = pltpu.VMEM((tokens, 2 * HD), jnp.bfloat16)
    params = pltpu.CompilerParams(vmem_limit_bytes=VMEM)

    def kv_specs(h):
        kk, vv, j = other[h]
        mine_spec, far_spec = pl.BlockSpec(head_block, column(h)), pl.BlockSpec(head_block, column(j))
        return [mine_spec, far_spec, mine_spec, far_spec], (k, kk, v, vv)

    def own_call(h):
        specs, arrays = kv_specs(h)
        result = pl.pallas_call(
            functools.partial(own_kernel, ring),
            grid=(1,),
            in_specs=[SMEM, pl.BlockSpec(head_block, column(h))] + specs,
            out_specs=[full, full] + [piece] * ring,
            out_shape=[wide, wide] + [small] * ring,
            scratch_shapes=[extended, extended],
            compiler_params=params,
            cost_estimate=cost(1, 2 * 2**20),
            name="own_%d" % h,
        )(ints, q, *arrays)
        return result[0], result[1], result[2:]

    def step_call(h, xq, following):
        specs, arrays = kv_specs(h)
        result = pl.pallas_call(
            functools.partial(step_kernel, ring),
            grid=(2,),
            in_specs=[SMEM, full, pl.BlockSpec(head_block, column(h))]
            + specs
            + [pl.BlockSpec(head_block, column(following))],
            out_specs=[full, pl.BlockSpec((tokens // HD, HD), fixed), full, full] + [piece] * ring,
            out_shape=[thin, levels, wide, wide] + [small] * ring,
            scratch_shapes=[extended, extended],
            compiler_params=params,
            cost_estimate=cost(2, 3 * 2**20),
            name="step_%d" % h,
        )(ints, xq, q, *arrays, q)
        return result[0], result[1], result[2], result[3], result[4:]

    def merge_call(h, own, lse, pieces, r, rl):
        return pl.pallas_call(
            functools.partial(merge_kernel, ring),
            in_specs=[SMEM, SMEM] + [ANY] * (4 + ring),
            out_specs=[ANY] * ring,
            out_shape=[small] * ring,
            input_output_aliases={6 + d: d for d in range(ring)},
            scratch_shapes=[
                pltpu.VMEM(head_block, jnp.float32), pltpu.VMEM(head_block, jnp.float32),
                pltpu.VMEM(head_block, jnp.bfloat16), pltpu.VMEM((tokens // HD, HD), jnp.float32),
                pltpu.VMEM((ring, piece_rows, HD), jnp.bfloat16), pltpu.SemaphoreType.DMA((max(4, ring),)),
            ],
            compiler_params=params,
            cost_estimate=cost(0.3, 2**20),
            name="merge_%d" % h,
        )(ints, shift, own, lse, r, rl, *pieces)

    def far_call(h, own, lse, pieces, far):
        return pl.pallas_call(
            functools.partial(far_kernel, ring, h),
            in_specs=[SMEM, SMEM] + [ANY] * (7 + ring),
            out_specs=[ANY] * ring,
            out_shape=[small] * ring,
            input_output_aliases={9 + d: d for d in range(ring)},
            scratch_shapes=[
                pltpu.VMEM(head_block, jnp.float32), pltpu.VMEM(head_block, jnp.float32),
            ]
            + [pltpu.VMEM(head_block, jnp.bfloat16)] * 5
            + [
                extended, extended,
                pltpu.VMEM((ring, piece_rows, HD), jnp.bfloat16), pltpu.SemaphoreType.DMA((max(7, ring),)),
            ],
            compiler_params=params,
            cost_estimate=cost(1, 3 * 2**20),
            name="far_%d" % h,
        )(ints, shift, own, lse, q, *far, *pieces)

    def spread(pieces):
        return [pieces[0]] + [
            lax.ppermute(pieces[d], "seq", [(i, (i + d) % ring) for i in range(ring)]) for d in range(1, ring)
        ]

    def place_call(order, landed, before):
        parts = [p for h in order for p in landed[h]]
        extra = [] if before is None else [before]
        return pl.pallas_call(
            functools.partial(place_kernel, order, ring, heads, before is None),
            in_specs=[SMEM] + [ANY] * (len(parts) + len(extra)),
            out_specs=ANY,
            out_shape=jax.ShapeDtypeStruct((piece_rows, ring * width), jnp.bfloat16),
            input_output_aliases={} if before is None else {1 + len(parts): 0},
            scratch_shapes=[pltpu.SemaphoreType.DMA((len(parts),))],
            compiler_params=params,
            cost_estimate=cost(0.1, 2**20),
            name="place_%d" % order[0],
        )(ints, *parts, *extra)

    landed = {}
    owned = {h: own_call(h) for h in far_heads}
    arrived = list(first)
    arrived_levels = [None] * lag
    state = {}
    for i, h in enumerate(near_heads):
        send, send_lse, own, lse, pieces = step_call(h, arrived[i], min(i + lag, heads - 3))
        state[h] = (own, lse, pieces)
        arrived.append(lax.ppermute(send, "span", swap))
        arrived_levels.append(lax.ppermute(send_lse, "span", swap))
    for n, h in enumerate(far_heads):
        kk, vv = arrived[2 * n], arrived[2 * n + 1]
        far = (kk, lax.ppermute(kk, "head", swap), vv, lax.ppermute(vv, "head", swap))
        own, lse, pieces = owned[h]
        landed[h] = spread(far_call(h, own, lse, pieces, far))
    for i, h in enumerate(near_heads):
        own, lse, pieces = state[h]
        landed[h] = spread(merge_call(h, own, lse, pieces, arrived[lag + i], arrived_levels[lag + i]))
    order = far_heads + near_heads
    result = place_call(order[:-2], landed, None)
    result = place_call(order[-2:], landed, result)
    return result.reshape(1, 1, piece_rows, ring * width)


def solution(mesh):
    def per_device(queries, keys, values, span_order):
        paired = lax.axis_size("span") == 2 and lax.axis_size("head") == 2
        if paired and queries.shape[3] // HD >= 6:
            return staggered(queries, keys, values, span_order)
        return gathered(queries, keys, values, span_order)

    return jax.shard_map(
        per_device,
        mesh=mesh,
        in_specs=(
            P(("rep", "span"), "head", None, "seq"),
            P(("rep", "span"), "head", None, "seq"),
            P(("rep", "span"), "head", None, "seq"),
            P("rep"),
        ),
        out_specs=P(("rep", "span"), "head", "seq", None),
        check_vma=False,
    )
```

```python
import functools
import math

import jax
import jax.numpy as jnp
from jax import lax
from jax.experimental import pallas as pl
from jax.experimental.pallas import tpu as pltpu
from jax.sharding import PartitionSpec as P

HD = 128
LOG2E = math.log2(math.e)
SCALE2 = LOG2E / math.sqrt(HD)
ROWS = 512
VMEM = 24 * 2**20
ANY = pl.BlockSpec(memory_space=pl.ANY)
SMEM = pl.BlockSpec(memory_space=pltpu.SMEM)
LOCAL = pl.BlockSpec(memory_space=pltpu.VMEM)


def lookup(span_order, block_index):
    table = jnp.arange(span_order.shape[0], dtype=jnp.int32)
    return jnp.sum(
        jnp.where(block_index[:, None] == table[None, :], span_order[None, :], 0), axis=1
    )


def initial(query_heads):
    query_count = query_heads.shape[0]
    local_heads = query_heads.shape[1]
    return (
        jnp.full((local_heads, query_count), -1e30, jnp.float32),
        jnp.zeros((local_heads, query_count), jnp.float32),
        jnp.zeros((local_heads, query_count, HD), jnp.float32),
    )


def attend(running, query_heads, key_piece, value_piece, block_span, own_span, bias_rate):
    block_count = key_piece.shape[0]
    piece_rows = key_piece.shape[1]
    local_heads = key_piece.shape[2] // HD
    key_count = block_count * piece_rows
    score_scale = 1.0 / math.sqrt(HD)
    key_spans = jnp.repeat(block_span, piece_rows)
    allowed = key_spans <= own_span
    distance_bias = (own_span - key_spans).astype(jnp.float32) * jnp.float32(bias_rate)
    block_size = 1024
    block_total = key_count // block_size
    key_blocks = key_piece.reshape(block_total, block_size, local_heads, HD)
    value_blocks = value_piece.reshape(block_total, block_size, local_heads, HD)
    allow_blocks = allowed.reshape(block_total, block_size)
    bias_blocks = distance_bias.reshape(block_total, block_size)

    def advance(status, block_item):
        key_block, value_block, allow_block, bias_block = block_item
        maxima, totals, weighted = status
        scores = (
            jnp.einsum("qhd,khd->hqk", query_heads, key_block, preferred_element_type=jnp.float32)
            * score_scale
        )
        scores = scores - bias_block[None, None, :]
        scores = jnp.where(allow_block[None, None, :], scores, jnp.float32(-1e30))
        new_max = jnp.maximum(maxima, jnp.max(scores, axis=2))
        weights = jnp.where(
            allow_block[None, None, :], jnp.exp(scores - new_max[:, :, None]), 0.0
        ).astype(jnp.bfloat16)
        shrink = jnp.exp(maxima - new_max)
        totals = totals * shrink + jnp.sum(weights.astype(jnp.float32), axis=2)
        weighted = weighted * shrink[:, :, None] + jnp.einsum(
            "hqk,khd->hqd", weights, value_block, preferred_element_type=jnp.float32
        )
        return ((new_max, totals, weighted), None)

    running, unused = lax.scan(
        advance, running, (key_blocks, value_blocks, allow_blocks, bias_blocks)
    )
    return running


def finish(running):
    maxima, totals, weighted = running
    local_heads = weighted.shape[0]
    query_count = weighted.shape[1]
    output = (weighted / totals[:, :, None]).transpose(1, 0, 2)
    return output.reshape(1, 1, query_count, local_heads * HD).astype(jnp.bfloat16)


def gathered(queries, keys, values, span_order):
    half_rows = queries.shape[2]
    local_width = queries.shape[3]
    local_heads = local_width // HD
    halves = lax.axis_size("head")
    bias_rate = 1.0 / (2.0 * span_order.shape[0])
    own_span = lookup(span_order, jnp.reshape(lax.axis_index("span"), (1,)))[0]
    query_heads = queries.reshape(half_rows, local_heads, HD)
    pieces = (
        lax.all_gather(keys, ("span", "head"), axis=0, tiled=True),
        lax.all_gather(values, ("span", "head"), axis=0, tiled=True),
    )
    count = pieces[0].shape[0]
    block_index = jnp.arange(count, dtype=jnp.int32) // halves
    key_piece = pieces[0].reshape(count, half_rows, local_width)
    value_piece = pieces[1].reshape(count, half_rows, local_width)
    running = attend(
        initial(query_heads),
        query_heads,
        key_piece,
        value_piece,
        lookup(span_order, block_index),
        own_span,
        bias_rate,
    )
    result = finish(running)
    return lax.all_to_all(result, "seq", split_axis=2, concat_axis=3, tiled=True)


def rows_by_cols(a, b):
    return lax.dot_general(a, b, (((1,), (1,)), ((), ())), preferred_element_type=jnp.float32)


def attend_rows(q, k0, k1, v0, v1):
    parts = []
    for k, v in ((k0, v0), (k1, v1)):
        scores = rows_by_cols(q, k[...])
        top = jnp.max(scores, axis=1, keepdims=True) * SCALE2
        weights = jnp.exp2(scores * SCALE2 - top).astype(jnp.bfloat16)
        parts.append((jnp.dot(weights, v[...], preferred_element_type=jnp.float32), top))
    (a0, m0), (a1, m1) = parts
    top = jnp.maximum(m0, m1)
    both = a0 * jnp.exp2(m0 - top) + a1 * jnp.exp2(m1 - top)
    return both[:, :HD], both[:, HD:], top


def roles(order):
    group = lax.axis_index("span")
    behind = order[group] - order[1 - group]
    bias_rate = LOG2E / (2.0 * order.shape[0])
    return behind > 0, lax.axis_index("seq"), behind.astype(jnp.float32) * jnp.float32(bias_rate)


def load_values(v0, v1, e0, e1):
    e0[:, :HD] = v0
    e1[:, :HD] = v1


def fill_ones(e0, e1):
    for e in (e0, e1):
        e[:, HD:] = jnp.ones_like(e[:, HD:])


def put_pieces(me, own, pieces):
    count = len(pieces)
    size = pieces[0].shape[0]
    for d, piece in enumerate(pieces):
        start = pl.multiple_of(lax.rem(me + d, count) * size, size)
        piece[...] = own[pl.ds(start, size), :].astype(jnp.bfloat16)


def span_of(part, count=1):
    return pl.ds(part * HD, count * HD)


def own_kernel(pieces, after, head, ks, vs, order, q, k0, k1, v0, v1, *rest):
    own, lse = rest[after : after + 2]
    out, (e0, e1) = rest[after + 2 : after + 2 + pieces], rest[after + 2 + pieces :]
    unused_high, me, unused_shift = roles(order)
    fill_ones(e0, e1)
    for p in range(2):
        cols = span_of(p)
        load_values(v0[:, span_of(head + p)], v1[:, span_of(vs + p)], e0, e1)
        for r in range(0, q.shape[0], ROWS):
            rows = pl.ds(r, ROWS)
            o, l, m = attend_rows(
                q[rows, span_of(head + p)], k0.at[:, span_of(head + p)], k1.at[:, span_of(ks + p)], e0, e1
            )
            own[rows, cols] = o / l
            lse[rows, cols] = m + jnp.log2(l)
    put_pieces(me, own, out)


def cross_kernel(after, following, head, ks, vs, order, xq, q, k0, k1, v0, v1, *rest):
    send, e0, e1 = rest[after:]
    tokens = k0.shape[0]
    high, unused_me, unused_shift = roles(order)

    if following is not None:
        @pl.when(high)
        def _():
            send[pl.ds(0, tokens), :] = q[:, span_of(following, 2)]

    @pl.when(jnp.logical_not(high))
    def _():
        fill_ones(e0, e1)
        for p in range(2):
            cols = span_of(p)
            load_values(v0[:, span_of(head + p)], v1[:, span_of(vs + p)], e0, e1)
            levels = []
            for r in range(0, tokens, ROWS):
                o, l, m = attend_rows(
                    xq[pl.ds(r, ROWS), cols], k0.at[:, span_of(head + p)], k1.at[:, span_of(ks + p)], e0, e1
                )
                send[pl.ds(r, ROWS), cols] = (o / l).astype(jnp.bfloat16)
                level = m + jnp.log2(l)
                levels += [level[c : c + HD, :].T[:1, :] for c in range(0, ROWS, HD)]
            level = jnp.concatenate(levels, axis=0)
            terms = []
            for _ in range(3):
                term = level.astype(jnp.bfloat16).astype(jnp.float32)
                level = level - term
                terms.append(term)
            terms.append(jnp.zeros_like(level))
            send[pl.ds(tokens, 4 * len(levels)), cols] = jnp.concatenate(terms, axis=0).astype(jnp.bfloat16)


def blend(o0, l0, o1, l1):
    top = jnp.maximum(l0, l1)
    w0, w1 = jnp.exp2(l0 - top), jnp.exp2(l1 - top)
    return (o0 * w0 + o1 * w1) / (w0 + w1)


def copy_in(pairs, sems):
    copies = [pltpu.make_async_copy(s, d, sems.at[i]) for i, (s, d) in enumerate(pairs)]
    for c in copies:
        c.start()
    for c in copies:
        c.wait()


def merge_kernel(pieces, after, order, own, lse, r, *rest):
    rest = rest[pieces + after :]
    out, (both,) = rest[:pieces], rest[pieces:]
    tokens, width = own.shape
    high, me, shift = roles(order)

    @pl.when(high)
    def _():
        count = tokens // HD
        for c in range(0, width, HD):
            cols = pl.ds(c, HD)
            terms = r[pl.ds(tokens, 4 * count), cols].astype(jnp.float32)
            level = terms[:count] + terms[count : 2 * count] + terms[2 * count : 3 * count]
            for i in range(count):
                rows = pl.ds(i * HD, HD)
                far = jnp.broadcast_to(level[i : i + 1, :], (HD, HD)).T - shift
                both[rows, cols] = blend(own[rows, cols], lse[rows, cols], r[rows, cols].astype(jnp.float32), far)
        put_pieces(me, both, out)


def far_kernel(pieces, after, head, part, order, own, lse, q, x0, x1, *rest):
    rest = rest[pieces + after :]
    out, (e0, e1, both) = rest[:pieces], rest[pieces:]
    cols = span_of(part)
    high, me, shift = roles(order)

    @pl.when(high)
    def _():
        fill_ones(e0, e1)
        load_values(x0[:, span_of(1)], x1[:, span_of(1)], e0, e1)
        for i in range(0, own.shape[0], ROWS):
            rows = pl.ds(i, ROWS)
            o, l, m = attend_rows(q[rows, span_of(head)], x0.at[:, span_of(0)], x1.at[:, span_of(0)], e0, e1)
            level = m + jnp.log2(l) - shift
            both[rows, :] = blend(own[rows, cols], lse[rows, cols], o / l, level)
        put_pieces(me, both, [piece.at[:, cols] for piece in out])


def place_kernel(heads, pieces, total, after, order, *rest):
    parts, rest = rest[: len(heads) * pieces], rest[len(heads) * pieces :]
    out, sems = rest[-2:]
    unused_high, me, unused_shift = roles(order)
    pairs = []
    for a, h in enumerate(heads):
        for d in range(pieces):
            part = parts[a * pieces + d]
            source = lax.rem(me + (pieces - d), pieces)
            start = pl.multiple_of((source * total + h) * HD, HD)
            pairs.append((part, out.at[:, pl.ds(start, part.shape[1])]))
    copy_in(pairs, sems)


def first_kernel(far, order, q, k, v, x0, x1, g0, g1, qv, kv, vv, sems):
    cols = span_of
    high, unused_me, unused_shift = roles(order)
    copy_in([(k, kv), (v, vv), (q, qv)], sems)
    for g, h in ((g0, far), (g1, 0)):
        g[:, cols(0, 2)] = kv[:, cols(h, 2)]
        g[:, cols(2, 2)] = vv[:, cols(h, 2)]

    @pl.when(high)
    def _():
        for i, x in enumerate((x0, x1)):
            x[...] = qv[:, cols(2 * i, 2)]

    @pl.when(jnp.logical_not(high))
    def _():
        for i, x in enumerate((x0, x1)):
            x[:, cols(0)] = kv[:, cols(far + i)]
            x[:, cols(1)] = vv[:, cols(far + i)]


def cost(units, size):
    return pl.CostEstimate(flops=int(units * 3e9), bytes_accessed=size, transcendentals=0)


def staggered(queries, keys, values, span_order):
    q, k, v = queries[0, 0], keys[0, 0], values[0, 0]
    tokens, width = q.shape
    heads = width // HD
    ring = lax.axis_size("seq")
    piece_rows = tokens // ring
    swap = [(0, 1), (1, 0)]
    far = heads - 2
    near = list(range(0, far, 2))
    lag = 2

    params = pltpu.CompilerParams(vmem_limit_bytes=VMEM)
    sent_rows = tokens + 4 * (tokens // HD)
    wide = jax.ShapeDtypeStruct((tokens, 2 * HD), jnp.float32)
    two = jax.ShapeDtypeStruct((tokens, 2 * HD), jnp.bfloat16)
    four = jax.ShapeDtypeStruct((tokens, 4 * HD), jnp.bfloat16)
    small = jax.ShapeDtypeStruct((piece_rows, 2 * HD), jnp.bfloat16)
    whole = jax.ShapeDtypeStruct(q.shape, jnp.bfloat16)
    extended = pltpu.VMEM((tokens, 2 * HD), jnp.bfloat16)

    def swapped(a, axis):
        return lax.ppermute(a, axis, swap)

    x0, x1, group, g0, q, k, v = pl.pallas_call(
        functools.partial(first_kernel, far),
        in_specs=[SMEM] + [ANY] * 3,
        out_specs=[LOCAL] * 7,
        out_shape=[two, two, four, four, whole, whole, whole],
        scratch_shapes=[pltpu.SemaphoreType.DMA((3,))],
        compiler_params=params,
        cost_estimate=cost(0, 6 * 2**20),
        name="first",
    )(span_order, q, k, v)
    arrived = [swapped(x0, "span"), swapped(x1, "span")]
    group, g0 = swapped(group, "head"), swapped(g0, "head")
    k_far, v_far = swapped(k, "head"), swapped(v, "head")
    other = {far: (group, 0, group, 2), 0: (g0, 0, g0, 2)}
    for h in near[1:]:
        other[h] = (k_far, h, v_far, h)

    def own_call(h, after):
        kk, ks, vv, vs = other[h]
        result = pl.pallas_call(
            functools.partial(own_kernel, ring, len(after), h, ks, vs),
            in_specs=[SMEM] + [LOCAL] * 5 + [ANY] * len(after),
            out_specs=[LOCAL] * (2 + ring),
            out_shape=[wide, wide] + [small] * ring,
            scratch_shapes=[extended, extended],
            compiler_params=params,
            cost_estimate=cost(2, 3 * 2**20),
            name="own_%d" % h,
        )(span_order, q, k, kk, v, vv, *after)
        return result[0], result[1], result[2:]

    def cross_call(h, xq, following, after):
        kk, ks, vv, vs = other[h]
        return pl.pallas_call(
            functools.partial(cross_kernel, len(after), following, h, ks, vs),
            in_specs=[SMEM] + [LOCAL] * 6 + [ANY] * len(after),
            out_specs=LOCAL,
            out_shape=jax.ShapeDtypeStruct((sent_rows, 2 * HD), jnp.bfloat16),
            scratch_shapes=[extended, extended],
            compiler_params=params,
            cost_estimate=cost(2, 3 * 2**20),
            name="cross_%d" % h,
        )(span_order, xq, q, k, kk, v, vv, *after)

    def merge_call(h, own, lse, pieces, r, after):
        return pl.pallas_call(
            functools.partial(merge_kernel, ring, len(after)),
            in_specs=[SMEM] + [LOCAL] * (3 + ring) + [ANY] * len(after),
            out_specs=[LOCAL] * ring,
            out_shape=[small] * ring,
            input_output_aliases={4 + d: d for d in range(ring)},
            scratch_shapes=[pltpu.VMEM((tokens, 2 * HD), jnp.float32)],
            compiler_params=params,
            cost_estimate=cost(0.4, 2**20),
            name="merge_%d" % h,
        )(span_order, own, lse, r, *pieces, *after)

    def far_call(part, own, lse, pieces, x, after):
        return pl.pallas_call(
            functools.partial(far_kernel, ring, len(after), far + part, part),
            in_specs=[SMEM] + [LOCAL] * (5 + ring) + [ANY] * len(after),
            out_specs=[LOCAL] * ring,
            out_shape=[small] * ring,
            input_output_aliases={6 + d: d for d in range(ring)},
            scratch_shapes=[extended, extended, pltpu.VMEM((tokens, HD), jnp.float32)],
            compiler_params=params,
            cost_estimate=cost(1, 3 * 2**20),
            name="far_%d" % part,
        )(span_order, own, lse, q, *x, *pieces, *after)

    def spread(pieces):
        return [pieces[0]] + [
            lax.ppermute(pieces[d], "seq", [(i, (i + d) % ring) for i in range(ring)]) for d in range(1, ring)
        ]

    def place_call(order, landed, before, after):
        parts = [p for h in order for p in landed[h]]
        extra = list(after) + ([] if before is None else [before])
        return pl.pallas_call(
            functools.partial(place_kernel, order, ring, heads, len(after)),
            in_specs=[SMEM] + [ANY] * (len(parts) + len(extra)),
            out_specs=ANY,
            out_shape=jax.ShapeDtypeStruct((piece_rows, ring * width), jnp.bfloat16),
            input_output_aliases={} if before is None else {len(parts) + len(extra): 0},
            scratch_shapes=[pltpu.SemaphoreType.DMA((len(parts),))],
            compiler_params=params,
            cost_estimate=cost(0.1, 2**20),
            name="place_%d" % order[0],
        )(span_order, *parts, *extra)

    def send_on(i, h, after):
        follows = h + 2 * lag
        r = cross_call(h, arrived[i], follows if follows < far else None, after)
        arrived.append(swapped(r, "span"))
        return r

    owned, landed = {}, {}
    owned[far] = own_call(far, [])
    owned[0] = own_call(0, [owned[far][0]])
    done = owned[0][0]
    far_own, far_lse, pieces = owned[far]
    for part in range(2):
        held, unused = lax.optimization_barrier((arrived[part], done))
        both = (held, swapped(held, "head"))
        done = send_on(part, near[part], [done])
        pieces = far_call(part, far_own, far_lse, pieces, both, [done])
        done = pieces[0]
    landed[far] = spread(pieces)
    for i in range(lag, len(near)):
        done = send_on(i, near[i], [done])
    result, waiting = None, far
    for i, h in enumerate(near):
        if h not in owned:
            result = place_call([waiting], landed, result, [done])
            waiting = near[i - 1]
            owned[h] = own_call(h, [done, result])
            done = owned[h][0]
        pieces = merge_call(h, *owned[h], arrived[lag + i], [done])
        done = pieces[0]
        landed[h] = spread(pieces)
    result = place_call([waiting], landed, result, [done])
    result = place_call([near[-1]], landed, result, [])
    return result.reshape(1, 1, piece_rows, ring * width)


def solution(mesh):
    def per_device(queries, keys, values, span_order):
        paired = lax.axis_size("span") == 2 and lax.axis_size("head") == 2
        heads = queries.shape[3] // HD
        if paired and heads >= 6 and heads % 2 == 0:
            return staggered(queries, keys, values, span_order)
        return gathered(queries, keys, values, span_order)

    return jax.shard_map(
        per_device,
        mesh=mesh,
        in_specs=(
            P(("rep", "span"), "head", None, "seq"),
            P(("rep", "span"), "head", None, "seq"),
            P(("rep", "span"), "head", None, "seq"),
            P("rep"),
        ),
        out_specs=P(("rep", "span"), "head", "seq", None),
        check_vma=False,
    )
```

```python
import functools
import math

import jax
import jax.numpy as jnp
from jax import lax
from jax.experimental import pallas as pl
from jax.experimental.pallas import tpu as pltpu
from jax.sharding import PartitionSpec as P

HD = 128
LOG2E = math.log2(math.e)
SCALE2 = LOG2E / math.sqrt(HD)
ROWS = 512
VMEM = 24 * 2**20
ANY = pl.BlockSpec(memory_space=pl.ANY)
SMEM = pl.BlockSpec(memory_space=pltpu.SMEM)
LOCAL = pl.BlockSpec(memory_space=pltpu.VMEM)
HBM = pl.BlockSpec(memory_space=pltpu.HBM)


def lookup(span_order, block_index):
    table = jnp.arange(span_order.shape[0], dtype=jnp.int32)
    return jnp.sum(
        jnp.where(block_index[:, None] == table[None, :], span_order[None, :], 0), axis=1
    )


def initial(query_heads):
    query_count = query_heads.shape[0]
    local_heads = query_heads.shape[1]
    return (
        jnp.full((local_heads, query_count), -1e30, jnp.float32),
        jnp.zeros((local_heads, query_count), jnp.float32),
        jnp.zeros((local_heads, query_count, HD), jnp.float32),
    )


def attend(running, query_heads, key_piece, value_piece, block_span, own_span, bias_rate):
    block_count = key_piece.shape[0]
    piece_rows = key_piece.shape[1]
    local_heads = key_piece.shape[2] // HD
    key_count = block_count * piece_rows
    score_scale = 1.0 / math.sqrt(HD)
    key_spans = jnp.repeat(block_span, piece_rows)
    allowed = key_spans <= own_span
    distance_bias = (own_span - key_spans).astype(jnp.float32) * jnp.float32(bias_rate)
    block_size = 1024
    block_total = key_count // block_size
    key_blocks = key_piece.reshape(block_total, block_size, local_heads, HD)
    value_blocks = value_piece.reshape(block_total, block_size, local_heads, HD)
    allow_blocks = allowed.reshape(block_total, block_size)
    bias_blocks = distance_bias.reshape(block_total, block_size)

    def advance(status, block_item):
        key_block, value_block, allow_block, bias_block = block_item
        maxima, totals, weighted = status
        scores = (
            jnp.einsum("qhd,khd->hqk", query_heads, key_block, preferred_element_type=jnp.float32)
            * score_scale
        )
        scores = scores - bias_block[None, None, :]
        scores = jnp.where(allow_block[None, None, :], scores, jnp.float32(-1e30))
        new_max = jnp.maximum(maxima, jnp.max(scores, axis=2))
        weights = jnp.where(
            allow_block[None, None, :], jnp.exp(scores - new_max[:, :, None]), 0.0
        ).astype(jnp.bfloat16)
        shrink = jnp.exp(maxima - new_max)
        totals = totals * shrink + jnp.sum(weights.astype(jnp.float32), axis=2)
        weighted = weighted * shrink[:, :, None] + jnp.einsum(
            "hqk,khd->hqd", weights, value_block, preferred_element_type=jnp.float32
        )
        return ((new_max, totals, weighted), None)

    running, unused = lax.scan(
        advance, running, (key_blocks, value_blocks, allow_blocks, bias_blocks)
    )
    return running


def finish(running):
    maxima, totals, weighted = running
    local_heads = weighted.shape[0]
    query_count = weighted.shape[1]
    output = (weighted / totals[:, :, None]).transpose(1, 0, 2)
    return output.reshape(1, 1, query_count, local_heads * HD).astype(jnp.bfloat16)


def gathered(queries, keys, values, span_order):
    half_rows = queries.shape[2]
    local_width = queries.shape[3]
    local_heads = local_width // HD
    halves = lax.axis_size("head")
    bias_rate = 1.0 / (2.0 * span_order.shape[0])
    own_span = lookup(span_order, jnp.reshape(lax.axis_index("span"), (1,)))[0]
    query_heads = queries.reshape(half_rows, local_heads, HD)
    pieces = (
        lax.all_gather(keys, ("span", "head"), axis=0, tiled=True),
        lax.all_gather(values, ("span", "head"), axis=0, tiled=True),
    )
    count = pieces[0].shape[0]
    block_index = jnp.arange(count, dtype=jnp.int32) // halves
    key_piece = pieces[0].reshape(count, half_rows, local_width)
    value_piece = pieces[1].reshape(count, half_rows, local_width)
    running = attend(
        initial(query_heads),
        query_heads,
        key_piece,
        value_piece,
        lookup(span_order, block_index),
        own_span,
        bias_rate,
    )
    result = finish(running)
    return lax.all_to_all(result, "seq", split_axis=2, concat_axis=3, tiled=True)


def rows_by_cols(a, b):
    return lax.dot_general(a, b, (((1,), (1,)), ((), ())), preferred_element_type=jnp.float32)


def attend_rows(q, k0, k1, v0, v1):
    parts = []
    for k, v in ((k0, v0), (k1, v1)):
        scores = rows_by_cols(q, k[...])
        top = jnp.max(scores, axis=1, keepdims=True) * SCALE2
        weights = jnp.exp2(scores * SCALE2 - top).astype(jnp.bfloat16)
        parts.append((jnp.dot(weights, v[...], preferred_element_type=jnp.float32), top))
    (a0, m0), (a1, m1) = parts
    top = jnp.maximum(m0, m1)
    both = a0 * jnp.exp2(m0 - top) + a1 * jnp.exp2(m1 - top)
    return both[:, :HD], both[:, HD:], top


def roles(order):
    group = lax.axis_index("span")
    behind = order[group] - order[1 - group]
    bias_rate = LOG2E / (2.0 * order.shape[0])
    return behind > 0, behind.astype(jnp.float32) * jnp.float32(bias_rate)


def load_values(v0, v1, e0, e1):
    e0[:, :HD] = v0
    e1[:, :HD] = v1


def fill_ones(e0, e1):
    for e in (e0, e1):
        e[:, HD:] = jnp.ones_like(e[:, HD:])


def put_pieces(own, out, layout):
    if layout is None:
        out[0][...] = own[...].astype(jnp.bfloat16)
        return
    me = lax.axis_index("seq")
    size = own.shape[0] // sum(len(ds) for ds in layout)
    for array, ds in zip(out, layout):
        for j, d in enumerate(ds):
            start = pl.multiple_of(lax.bitwise_xor(me, d) * size, size)
            array[pl.ds(j * size, size), :] = own[pl.ds(start, size), :].astype(jnp.bfloat16)


def span_of(part, count=1):
    return pl.ds(part * HD, count * HD)


ORDER = (
    "o0", "o1", "h0", "f0", "c1", "x1", "o2", "h1", "f1", "c2", "x2", "m1", "c3", "x3", "r0", "m2", "o3", "r1", "m3", "r2", "p01", "p2", "p3",
)
LAST = ((0,), (1,), (2,), (3,))
RELAYED = 3


def own_kernel(layout, after, head, order, q, k0, k1, v0, v1, *rest):
    own, lse, *out = rest[after:-2]
    e0, e1 = rest[-2:]
    fill_ones(e0, e1)
    for p in range(2):
        cols = span_of(p)
        load_values(v0[:, span_of(head + p)], v1[:, span_of(head + p)], e0, e1)
        for r in range(0, q.shape[0], ROWS):
            rows = pl.ds(r, ROWS)
            o, l, m = attend_rows(
                q[rows, span_of(head + p)], k0.at[:, span_of(head + p)], k1.at[:, span_of(head + p)], e0, e1
            )
            own[rows, cols] = o / l
            lse[rows, cols] = m + jnp.log2(l)
    put_pieces(own, out, layout)


def cross_kernel(after, following, head, order, xq, q, k0, k1, v0, v1, *rest):
    send, e0, e1 = rest[after:]
    tokens = q.shape[0]
    high, unused_shift = roles(order)

    if following is not None:
        @pl.when(high)
        def _():
            send[pl.ds(0, tokens), :] = q[:, span_of(following, 2)]

    @pl.when(jnp.logical_not(high))
    def _():
        fill_ones(e0, e1)
        for p in range(2):
            cols = span_of(p)
            load_values(v0[:, span_of(head + p)], v1[:, span_of(head + p)], e0, e1)
            levels = []
            for r in range(0, tokens, ROWS):
                o, l, m = attend_rows(
                    xq[pl.ds(r, ROWS), cols], k0.at[:, span_of(head + p)], k1.at[:, span_of(head + p)], e0, e1
                )
                send[pl.ds(r, ROWS), cols] = (o / l).astype(jnp.bfloat16)
                level = m + jnp.log2(l)
                levels += [level[c : c + HD, :].T[:1, :] for c in range(0, ROWS, HD)]
            level = jnp.concatenate(levels, axis=0)
            terms = []
            for _ in range(3):
                term = level.astype(jnp.bfloat16).astype(jnp.float32)
                level = level - term
                terms.append(term)
            terms.append(jnp.zeros_like(level))
            send[pl.ds(tokens, 4 * len(levels)), cols] = jnp.concatenate(terms, axis=0).astype(jnp.bfloat16)


def blend(o0, l0, o1, l1):
    top = jnp.maximum(l0, l1)
    w0, w1 = jnp.exp2(l0 - top), jnp.exp2(l1 - top)
    return (o0 * w0 + o1 * w1) / (w0 + w1)


def copy_in(pairs, sems):
    copies = [pltpu.make_async_copy(s, d, sems.at[i]) for i, (s, d) in enumerate(pairs)]
    for c in copies:
        c.start()
    for c in copies:
        c.wait()


def merge_kernel(layout, after, order, own, lse, r, *rest):
    *out, both = rest[(len(layout) if layout else 1) + after :]
    tokens, width = own.shape
    high, shift = roles(order)

    @pl.when(high)
    def _():
        count = tokens // HD
        for c in range(0, width, HD):
            cols = pl.ds(c, HD)
            terms = r[pl.ds(tokens, 4 * count), cols].astype(jnp.float32)
            level = terms[:count] + terms[count : 2 * count] + terms[2 * count : 3 * count]
            for i in range(count):
                rows = pl.ds(i * HD, HD)
                far = jnp.broadcast_to(level[i : i + 1, :], (HD, HD)).T - shift
                both[rows, cols] = blend(own[rows, cols], lse[rows, cols], r[rows, cols].astype(jnp.float32), far)
        put_pieces(both, out, layout)


def far_kernel(layout, after, head, part, order, own, lse, q, x0, x1, *rest):
    *out, e0, e1, both = rest[len(layout) + after :]
    cols = span_of(part)
    high, shift = roles(order)

    @pl.when(high)
    def _():
        fill_ones(e0, e1)
        load_values(x0[:, span_of(1)], x1[:, span_of(1)], e0, e1)
        for i in range(0, own.shape[0], ROWS):
            rows = pl.ds(i, ROWS)
            o, l, m = attend_rows(q[rows, span_of(head)], x0.at[:, span_of(0)], x1.at[:, span_of(0)], e0, e1)
            level = m + jnp.log2(l) - shift
            both[rows, :] = blend(own[rows, cols], lse[rows, cols], o / l, level)
        put_pieces(both, [piece.at[:, cols] for piece in out], layout)


def relay_kernel(after, near, got, *rest):
    out = rest[-1]
    size = out.shape[0] // 2
    out[pl.ds(0, size), :] = near[pl.ds(size, size), :]
    out[pl.ds(size, size), :] = got[pl.ds(size, size), :]


def place_kernel(count, items, total, *rest):
    arrays = rest[:count]
    out, sems = rest[-2:]
    me = lax.axis_index("seq")
    size = out.shape[0]
    pairs = []
    for i, row, d, h in items:
        start = row * total * HD + h * HD if d is None else pl.multiple_of((lax.bitwise_xor(me, d) * total + h) * HD, HD)
        pairs.append((arrays[i].at[pl.ds(row * size, size), :], out.at[:, pl.ds(start, arrays[i].shape[1])]))
    copy_in(pairs, sems)


def first_kernel(far, order, q, k, v, x0, x1, stage, sems):
    high, unused_shift = roles(order)

    @pl.when(high)
    def _():
        copy_in([(q.at[:, span_of(2 * i, 2)], stage.at[i]) for i in range(2)], sems)

    @pl.when(jnp.logical_not(high))
    def _():
        copy_in(
            [
                (a.at[:, span_of(far + i)], stage.at[i, :, span_of(j)])
                for i in range(2) for j, a in enumerate((k, v))
            ],
            sems,
        )

    copy_in([(stage.at[0], x0), (stage.at[1], x1)], sems)


def cost(units, size):
    return pl.CostEstimate(flops=int(units * 3e9), bytes_accessed=size, transcendentals=0)


def staggered(queries, keys, values, span_order):
    q, k, v = queries[0, 0], keys[0, 0], values[0, 0]
    tokens, width = q.shape
    heads = width // HD
    ring = lax.axis_size("seq")
    piece_rows = tokens // ring
    swap = [(0, 1), (1, 0)]
    far = heads - 2
    near = list(range(0, far, 2))
    lag = 2
    layouts = {h: ((0, 1), (2, 3)) if i < RELAYED else LAST for i, h in enumerate([far] + near)}

    params = pltpu.CompilerParams(vmem_limit_bytes=VMEM)
    sent_rows = tokens + 4 * (tokens // HD)
    wide = jax.ShapeDtypeStruct((tokens, 2 * HD), jnp.float32)
    two = jax.ShapeDtypeStruct((tokens, 2 * HD), jnp.bfloat16)
    extended = pltpu.VMEM((tokens, 2 * HD), jnp.bfloat16)

    def swapped(a, axis):
        return lax.ppermute(a, axis, swap)

    k_far, v_far = swapped(k, "head"), swapped(v, "head")
    x0, x1 = pl.pallas_call(
        functools.partial(first_kernel, far),
        in_specs=[SMEM] + [HBM] * 3,
        out_specs=[ANY] * 2,
        out_shape=[two, two],
        scratch_shapes=[pltpu.VMEM((2, tokens, 2 * HD), jnp.bfloat16), pltpu.SemaphoreType.DMA((4,))],
        compiler_params=params,
        cost_estimate=cost(0, 2 * 2**20),
        name="first",
    )(span_order, q, k, v)
    arrived = [swapped(x0, "span"), swapped(x1, "span")]

    def shapes(h):
        if layouts[h] is None:
            return [two]
        return [jax.ShapeDtypeStruct((len(ds) * piece_rows, 2 * HD), jnp.bfloat16) for ds in layouts[h]]

    def own_call(h, after):
        result = pl.pallas_call(
            functools.partial(own_kernel, layouts[h], len(after), h),
            in_specs=[SMEM] + [LOCAL] * 5 + [ANY] * len(after),
            out_specs=[LOCAL] * (2 + len(shapes(h))),
            out_shape=[wide, wide] + shapes(h),
            scratch_shapes=[extended, extended],
            compiler_params=params,
            cost_estimate=cost(2, 3 * 2**20),
            name="own_%d" % h,
        )(span_order, q, k, k_far, v, v_far, *after)
        return result[0], result[1], result[2:]

    def cross_call(h, xq, following, after):
        return pl.pallas_call(
            functools.partial(cross_kernel, len(after), following, h),
            in_specs=[SMEM] + [LOCAL] * 6 + [ANY] * len(after),
            out_specs=LOCAL,
            out_shape=jax.ShapeDtypeStruct((sent_rows, 2 * HD), jnp.bfloat16),
            scratch_shapes=[extended, extended],
            compiler_params=params,
            cost_estimate=cost(2, 3 * 2**20),
            name="cross_%d" % h,
        )(span_order, xq, q, k, k_far, v, v_far, *after)

    def merge_call(h, own, lse, pieces, r, after):
        return pl.pallas_call(
            functools.partial(merge_kernel, layouts[h], len(after)),
            in_specs=[SMEM] + [LOCAL] * (3 + len(pieces)) + [ANY] * len(after),
            out_specs=[LOCAL] * len(pieces),
            out_shape=shapes(h),
            input_output_aliases={4 + d: d for d in range(len(pieces))},
            scratch_shapes=[pltpu.VMEM((tokens, 2 * HD), jnp.float32)],
            compiler_params=params,
            cost_estimate=cost(0.4, 2**20),
            name="merge_%d" % h,
        )(span_order, own, lse, r, *pieces, *after)

    def far_call(part, own, lse, pieces, x, after):
        return pl.pallas_call(
            functools.partial(far_kernel, layouts[far], len(after), far + part, part),
            in_specs=[SMEM] + [LOCAL] * (5 + len(pieces)) + [ANY] * len(after),
            out_specs=[LOCAL] * len(pieces),
            out_shape=shapes(far),
            input_output_aliases={6 + d: d for d in range(len(pieces))},
            scratch_shapes=[extended, extended, pltpu.VMEM((tokens, HD), jnp.float32)],
            compiler_params=params,
            cost_estimate=cost(1, 3 * 2**20),
            name="far_%d" % part,
        )(span_order, own, lse, q, *x, *pieces, *after)

    def across(a, d):
        return lax.ppermute(a, "seq", [(i, i ^ d) for i in range(ring)])

    def start(h, pieces):
        if len(pieces) == ring:
            landed[h] = [(pieces[0], 0, 0)] + [(across(pieces[d], d), 0, d) for d in range(1, ring)]
        elif len(pieces) == 2:
            moving[h] = (pieces[0], across(pieces[1], 2))
        else:
            whole = lax.all_to_all(pieces[0], "seq", split_axis=0, concat_axis=0, tiled=True)
            landed[h] = [(whole, s, None) for s in range(ring)]

    def relay(h, done):
        near_rows, got = moving[h]
        both = pl.pallas_call(
            functools.partial(relay_kernel, 1),
            in_specs=[LOCAL] * 2 + [ANY],
            out_specs=LOCAL,
            out_shape=jax.ShapeDtypeStruct(got.shape, jnp.bfloat16),
            compiler_params=params,
            cost_estimate=cost(0.1, 2**19),
            name="relay_%d" % h,
        )(near_rows, got, done)
        last = across(both, 1)
        landed[h] = [(near_rows, 0, 0), (got, 0, 2), (last, 0, 1), (last, 1, 3)]
        return both

    def place(order, before, after):
        arrays, items = [], []
        for h in order:
            for a, row, d in landed[h]:
                found = [i for i, b in enumerate(arrays) if b is a]
                if not found:
                    arrays.append(a)
                items.append((found[0] if found else len(arrays) - 1, row, d, h))
        extra = list(after) + ([] if before is None else [before])
        return pl.pallas_call(
            functools.partial(place_kernel, len(arrays), items, heads),
            in_specs=[ANY] * (len(arrays) + len(extra)),
            out_specs=ANY,
            out_shape=jax.ShapeDtypeStruct((piece_rows, ring * width), jnp.bfloat16),
            input_output_aliases={} if before is None else {len(arrays) + len(extra) - 1: 0},
            scratch_shapes=[pltpu.SemaphoreType.DMA((len(items),))],
            compiler_params=params,
            cost_estimate=cost(0.1, 2**20),
            name="place_%d" % order[0],
        )(*arrays, *extra)

    def tie(a, b):
        return lax.optimization_barrier((a, b))[0]

    owned, moving, landed, results = {}, {}, {}, {}

    def own(h, done):
        owned[h] = own_call(h, [done] if done is not None else [])
        return owned[h][0]

    pairs = [far] + near
    far_heads, result, done = {}, None, None
    for op in ORDER:
        kind, i = op[0], int(op[1])
        if kind == "o":
            owned[pairs[i]] = own_call(pairs[i], [] if done is None else [done])
            done = owned[pairs[i]][0]
            if i == 0:
                far_pieces = owned[far][2]
        elif kind == "h":
            held = tie(arrived[i], done)
            far_heads[i] = (held, swapped(held, "head"))
        elif kind == "f":
            far_pieces = far_call(i, *owned[far][:2], far_pieces, far_heads[i], [done])
            done = far_pieces[0]
            if i == 1:
                start(far, far_pieces)
        elif kind == "c":
            xq = arrived[i - 1] if i <= lag else results[i - lag]
            follows = pairs[i + lag] if i + lag < len(pairs) else None
            results[i] = done = cross_call(pairs[i], xq, follows, [done])
        elif kind == "x":
            results[i] = swapped(results[i] if results[i] is done else tie(results[i], done), "span")
        elif kind == "m":
            pieces = merge_call(pairs[i], *owned[pairs[i]], results[i], [done])
            start(pairs[i], pieces)
            done = pieces[0]
        elif kind == "r":
            done = relay(pairs[i], done)
        elif kind == "p":
            result = place([pairs[int(j)] for j in op[1:]], result, [done] if done is not result else [])
            done = result
    return result.reshape(1, 1, piece_rows, ring * width)


def solution(mesh):
    def per_device(queries, keys, values, span_order):
        paired = lax.axis_size("span") == 2 and lax.axis_size("head") == 2
        if paired and lax.axis_size("seq") == 4 and queries.shape[3] == 8 * HD:
            return staggered(queries, keys, values, span_order)
        return gathered(queries, keys, values, span_order)

    return jax.shard_map(
        per_device,
        mesh=mesh,
        in_specs=(
            P(("rep", "span"), "head", None, "seq"),
            P(("rep", "span"), "head", None, "seq"),
            P(("rep", "span"), "head", None, "seq"),
            P("rep"),
        ),
        out_specs=P(("rep", "span"), "head", "seq", None),
        check_vma=False,
    )
```

```python
import functools
import math

import jax
import jax.numpy as jnp
from jax import lax
from jax.experimental import pallas as pl
from jax.experimental.pallas import tpu as pltpu
from jax.sharding import PartitionSpec as P

HD = 128
LOG2E = math.log2(math.e)
SCALE2 = LOG2E / math.sqrt(HD)
ROWS = 512
VMEM = 24 * 2**20
ANY = pl.BlockSpec(memory_space=pl.ANY)
SMEM = pl.BlockSpec(memory_space=pltpu.SMEM)
LOCAL = pl.BlockSpec(memory_space=pltpu.VMEM)
HBM = pl.BlockSpec(memory_space=pltpu.HBM)


def lookup(span_order, block_index):
    table = jnp.arange(span_order.shape[0], dtype=jnp.int32)
    return jnp.sum(
        jnp.where(block_index[:, None] == table[None, :], span_order[None, :], 0), axis=1
    )


def initial(query_heads):
    query_count = query_heads.shape[0]
    local_heads = query_heads.shape[1]
    return (
        jnp.full((local_heads, query_count), -1e30, jnp.float32),
        jnp.zeros((local_heads, query_count), jnp.float32),
        jnp.zeros((local_heads, query_count, HD), jnp.float32),
    )


def attend(running, query_heads, key_piece, value_piece, block_span, own_span, bias_rate):
    block_count = key_piece.shape[0]
    piece_rows = key_piece.shape[1]
    local_heads = key_piece.shape[2] // HD
    key_count = block_count * piece_rows
    score_scale = 1.0 / math.sqrt(HD)
    key_spans = jnp.repeat(block_span, piece_rows)
    allowed = key_spans <= own_span
    distance_bias = (own_span - key_spans).astype(jnp.float32) * jnp.float32(bias_rate)
    block_size = 1024
    block_total = key_count // block_size
    key_blocks = key_piece.reshape(block_total, block_size, local_heads, HD)
    value_blocks = value_piece.reshape(block_total, block_size, local_heads, HD)
    allow_blocks = allowed.reshape(block_total, block_size)
    bias_blocks = distance_bias.reshape(block_total, block_size)

    def advance(status, block_item):
        key_block, value_block, allow_block, bias_block = block_item
        maxima, totals, weighted = status
        scores = (
            jnp.einsum("qhd,khd->hqk", query_heads, key_block, preferred_element_type=jnp.float32)
            * score_scale
        )
        scores = scores - bias_block[None, None, :]
        scores = jnp.where(allow_block[None, None, :], scores, jnp.float32(-1e30))
        new_max = jnp.maximum(maxima, jnp.max(scores, axis=2))
        weights = jnp.where(
            allow_block[None, None, :], jnp.exp(scores - new_max[:, :, None]), 0.0
        ).astype(jnp.bfloat16)
        shrink = jnp.exp(maxima - new_max)
        totals = totals * shrink + jnp.sum(weights.astype(jnp.float32), axis=2)
        weighted = weighted * shrink[:, :, None] + jnp.einsum(
            "hqk,khd->hqd", weights, value_block, preferred_element_type=jnp.float32
        )
        return ((new_max, totals, weighted), None)

    running, unused = lax.scan(
        advance, running, (key_blocks, value_blocks, allow_blocks, bias_blocks)
    )
    return running


def finish(running):
    maxima, totals, weighted = running
    local_heads = weighted.shape[0]
    query_count = weighted.shape[1]
    output = (weighted / totals[:, :, None]).transpose(1, 0, 2)
    return output.reshape(1, 1, query_count, local_heads * HD).astype(jnp.bfloat16)


def gathered(queries, keys, values, span_order):
    half_rows = queries.shape[2]
    local_width = queries.shape[3]
    local_heads = local_width // HD
    halves = lax.axis_size("head")
    bias_rate = 1.0 / (2.0 * span_order.shape[0])
    own_span = lookup(span_order, jnp.reshape(lax.axis_index("span"), (1,)))[0]
    query_heads = queries.reshape(half_rows, local_heads, HD)
    pieces = (
        lax.all_gather(keys, ("span", "head"), axis=0, tiled=True),
        lax.all_gather(values, ("span", "head"), axis=0, tiled=True),
    )
    count = pieces[0].shape[0]
    block_index = jnp.arange(count, dtype=jnp.int32) // halves
    key_piece = pieces[0].reshape(count, half_rows, local_width)
    value_piece = pieces[1].reshape(count, half_rows, local_width)
    running = attend(
        initial(query_heads),
        query_heads,
        key_piece,
        value_piece,
        lookup(span_order, block_index),
        own_span,
        bias_rate,
    )
    result = finish(running)
    return lax.all_to_all(result, "seq", split_axis=2, concat_axis=3, tiled=True)


def rows_by_cols(a, b):
    return lax.dot_general(a, b, (((1,), (1,)), ((), ())), preferred_element_type=jnp.float32)


def attend_rows(q, k0, k1, v0, v1):
    parts = []
    for k, v in ((k0, v0), (k1, v1)):
        scores = rows_by_cols(q, k[...])
        top = jnp.max(scores, axis=1, keepdims=True) * SCALE2
        weights = jnp.exp2(scores * SCALE2 - top).astype(jnp.bfloat16)
        parts.append((jnp.dot(weights, v[...], preferred_element_type=jnp.float32), top))
    (a0, m0), (a1, m1) = parts
    top = jnp.maximum(m0, m1)
    both = a0 * jnp.exp2(m0 - top) + a1 * jnp.exp2(m1 - top)
    return both[:, :HD], both[:, HD:], top


def roles(order):
    group = lax.axis_index("span")
    behind = order[group] - order[1 - group]
    bias_rate = LOG2E / (2.0 * order.shape[0])
    return behind > 0, behind.astype(jnp.float32) * jnp.float32(bias_rate)


def load_values(v0, v1, e0, e1):
    e0[:, :HD] = v0
    e1[:, :HD] = v1


def fill_ones(e0, e1):
    for e in (e0, e1):
        e[:, HD:] = jnp.ones_like(e[:, HD:])


def put_pieces(own, out, layout):
    if layout is None:
        out[0][...] = own[...].astype(jnp.bfloat16)
        return
    me = lax.axis_index("seq")
    size = own.shape[0] // sum(len(ds) for ds in layout)
    for array, ds in zip(out, layout):
        for j, d in enumerate(ds):
            start = pl.multiple_of(lax.bitwise_xor(me, d) * size, size)
            array[pl.ds(j * size, size), :] = own[pl.ds(start, size), :].astype(jnp.bfloat16)


def span_of(part, count=1):
    return pl.ds(part * HD, count * HD)


ORDER = (
    "o0", "o1", "h0", "f0", "c1", "x1", "o2", "h1", "f1", "c2", "x2", "m1", "c3", "x3", "r0", "m2", "o3", "r1", "m3", "r2", "p01", "p2", "p3",
)
LAST = ((0,), (1,), (2,), (3,))
RELAYED = 3


def own_kernel(layout, after, head, order, q, k0, k1, v0, v1, *rest):
    own, lse, *out = rest[after:-2]
    e0, e1 = rest[-2:]
    for p in range(2):
        fill_ones(e0.at[p], e1.at[p])
        load_values(v0[:, span_of(head + p)], v1[:, span_of(head + p)], e0.at[p], e1.at[p])
    for p in range(2):
        cols = span_of(p)
        for r in range(0, q.shape[0], ROWS):
            rows = pl.ds(r, ROWS)
            o, l, m = attend_rows(
                q[rows, span_of(head + p)], k0.at[:, span_of(head + p)], k1.at[:, span_of(head + p)], e0.at[p], e1.at[p]
            )
            own[rows, cols] = o / l
            lse[rows, cols] = m + jnp.log2(l)
    put_pieces(own, out, layout)


def cross_kernel(after, following, head, order, xq, q, k0, k1, v0, v1, *rest):
    send, e0, e1 = rest[after:]
    tokens = q.shape[0]
    high, unused_shift = roles(order)

    if following is not None:
        @pl.when(high)
        def _():
            send[pl.ds(0, tokens), :] = q[:, span_of(following, 2)]

    @pl.when(jnp.logical_not(high))
    def _():
        for p in range(2):
            fill_ones(e0.at[p], e1.at[p])
            load_values(v0[:, span_of(head + p)], v1[:, span_of(head + p)], e0.at[p], e1.at[p])
        for p in range(2):
            cols = span_of(p)
            levels = []
            for r in range(0, tokens, ROWS):
                o, l, m = attend_rows(
                    xq[pl.ds(r, ROWS), cols], k0.at[:, span_of(head + p)], k1.at[:, span_of(head + p)], e0.at[p], e1.at[p]
                )
                send[pl.ds(r, ROWS), cols] = (o / l).astype(jnp.bfloat16)
                level = m + jnp.log2(l)
                levels += [level[c : c + HD, :].T[:1, :] for c in range(0, ROWS, HD)]
            level = jnp.concatenate(levels, axis=0)
            terms = []
            for _ in range(3):
                term = level.astype(jnp.bfloat16).astype(jnp.float32)
                level = level - term
                terms.append(term)
            terms.append(jnp.zeros_like(level))
            send[pl.ds(tokens, 4 * len(levels)), cols] = jnp.concatenate(terms, axis=0).astype(jnp.bfloat16)


def blend(o0, l0, o1, l1):
    top = jnp.maximum(l0, l1)
    w0, w1 = jnp.exp2(l0 - top), jnp.exp2(l1 - top)
    return (o0 * w0 + o1 * w1) / (w0 + w1)


def copy_in(pairs, sems):
    copies = [pltpu.make_async_copy(s, d, sems.at[i]) for i, (s, d) in enumerate(pairs)]
    for c in copies:
        c.start()
    for c in copies:
        c.wait()


def merge_kernel(layout, after, order, own, lse, r, *rest):
    *out, both = rest[(len(layout) if layout else 1) + after :]
    tokens, width = own.shape
    high, shift = roles(order)

    @pl.when(high)
    def _():
        count = tokens // HD
        for c in range(0, width, HD):
            cols = pl.ds(c, HD)
            terms = r[pl.ds(tokens, 4 * count), cols].astype(jnp.float32)
            level = terms[:count] + terms[count : 2 * count] + terms[2 * count : 3 * count]
            for i in range(count):
                rows = pl.ds(i * HD, HD)
                far = jnp.broadcast_to(level[i : i + 1, :], (HD, HD)).T - shift
                both[rows, cols] = blend(own[rows, cols], lse[rows, cols], r[rows, cols].astype(jnp.float32), far)
        put_pieces(both, out, layout)


def far_kernel(layout, after, head, part, order, own, lse, q, x0, x1, *rest):
    *out, e0, e1, both = rest[len(layout) + after :]
    cols = span_of(part)
    high, shift = roles(order)

    @pl.when(high)
    def _():
        fill_ones(e0, e1)
        load_values(x0[:, span_of(1)], x1[:, span_of(1)], e0, e1)
        for i in range(0, own.shape[0], ROWS):
            rows = pl.ds(i, ROWS)
            o, l, m = attend_rows(q[rows, span_of(head)], x0.at[:, span_of(0)], x1.at[:, span_of(0)], e0, e1)
            level = m + jnp.log2(l) - shift
            both[rows, :] = blend(own[rows, cols], lse[rows, cols], o / l, level)
        put_pieces(both, [piece.at[:, cols] for piece in out], layout)


def relay_kernel(after, near, got, *rest):
    out = rest[-1]
    size = out.shape[0] // 2
    out[pl.ds(0, size), :] = near[pl.ds(size, size), :]
    out[pl.ds(size, size), :] = got[pl.ds(size, size), :]


def place_kernel(count, items, total, *rest):
    arrays = rest[:count]
    out, sems = rest[-2:]
    me = lax.axis_index("seq")
    size = out.shape[0]
    pairs = []
    for i, row, d, h in items:
        start = row * total * HD + h * HD if d is None else pl.multiple_of((lax.bitwise_xor(me, d) * total + h) * HD, HD)
        pairs.append((arrays[i].at[pl.ds(row * size, size), :], out.at[:, pl.ds(start, arrays[i].shape[1])]))
    copy_in(pairs, sems)


def first_kernel(far, order, q, k, v, x0, x1, stage, sems):
    high, unused_shift = roles(order)

    @pl.when(high)
    def _():
        copy_in([(q.at[:, span_of(2 * i, 2)], stage.at[i]) for i in range(2)], sems)

    @pl.when(jnp.logical_not(high))
    def _():
        copy_in(
            [
                (a.at[:, span_of(far + i)], stage.at[i, :, span_of(j)])
                for i in range(2) for j, a in enumerate((k, v))
            ],
            sems,
        )

    copy_in([(stage.at[0], x0), (stage.at[1], x1)], sems)


def cost(units, size):
    return pl.CostEstimate(flops=int(units * 3e9), bytes_accessed=size, transcendentals=0)


def staggered(queries, keys, values, span_order):
    q, k, v = queries[0, 0], keys[0, 0], values[0, 0]
    tokens, width = q.shape
    heads = width // HD
    ring = lax.axis_size("seq")
    piece_rows = tokens // ring
    swap = [(0, 1), (1, 0)]
    far = heads - 2
    near = list(range(0, far, 2))
    lag = 2
    layouts = {h: ((0, 1), (2, 3)) if i < RELAYED else LAST for i, h in enumerate([far] + near)}

    params = pltpu.CompilerParams(vmem_limit_bytes=VMEM)
    sent_rows = tokens + 4 * (tokens // HD)
    wide = jax.ShapeDtypeStruct((tokens, 2 * HD), jnp.float32)
    two = jax.ShapeDtypeStruct((tokens, 2 * HD), jnp.bfloat16)
    extended = pltpu.VMEM((tokens, 2 * HD), jnp.bfloat16)
    both_extended = pltpu.VMEM((2, tokens, 2 * HD), jnp.bfloat16)

    def swapped(a, axis):
        return lax.ppermute(a, axis, swap)

    k_far, v_far = swapped(k, "head"), swapped(v, "head")
    x0, x1 = pl.pallas_call(
        functools.partial(first_kernel, far),
        in_specs=[SMEM] + [HBM] * 3,
        out_specs=[ANY] * 2,
        out_shape=[two, two],
        scratch_shapes=[pltpu.VMEM((2, tokens, 2 * HD), jnp.bfloat16), pltpu.SemaphoreType.DMA((4,))],
        compiler_params=params,
        cost_estimate=cost(0, 2 * 2**20),
        name="first",
    )(span_order, q, k, v)
    arrived = [swapped(x0, "span"), swapped(x1, "span")]

    def shapes(h):
        if layouts[h] is None:
            return [two]
        return [jax.ShapeDtypeStruct((len(ds) * piece_rows, 2 * HD), jnp.bfloat16) for ds in layouts[h]]

    def own_call(h, after):
        result = pl.pallas_call(
            functools.partial(own_kernel, layouts[h], len(after), h),
            in_specs=[SMEM] + [LOCAL] * 5 + [ANY] * len(after),
            out_specs=[LOCAL] * (2 + len(shapes(h))),
            out_shape=[wide, wide] + shapes(h),
            scratch_shapes=[both_extended, both_extended],
            compiler_params=params,
            cost_estimate=cost(2, 3 * 2**20),
            name="own_%d" % h,
        )(span_order, q, k, k_far, v, v_far, *after)
        return result[0], result[1], result[2:]

    def cross_call(h, xq, following, after):
        return pl.pallas_call(
            functools.partial(cross_kernel, len(after), following, h),
            in_specs=[SMEM] + [LOCAL] * 6 + [ANY] * len(after),
            out_specs=LOCAL,
            out_shape=jax.ShapeDtypeStruct((sent_rows, 2 * HD), jnp.bfloat16),
            scratch_shapes=[both_extended, both_extended],
            compiler_params=params,
            cost_estimate=cost(2, 3 * 2**20),
            name="cross_%d" % h,
        )(span_order, xq, q, k, k_far, v, v_far, *after)

    def merge_call(h, own, lse, pieces, r, after):
        return pl.pallas_call(
            functools.partial(merge_kernel, layouts[h], len(after)),
            in_specs=[SMEM] + [LOCAL] * (3 + len(pieces)) + [ANY] * len(after),
            out_specs=[LOCAL] * len(pieces),
            out_shape=shapes(h),
            input_output_aliases={4 + d: d for d in range(len(pieces))},
            scratch_shapes=[pltpu.VMEM((tokens, 2 * HD), jnp.float32)],
            compiler_params=params,
            cost_estimate=cost(0.4, 2**20),
            name="merge_%d" % h,
        )(span_order, own, lse, r, *pieces, *after)

    def far_call(part, own, lse, pieces, x, after):
        return pl.pallas_call(
            functools.partial(far_kernel, layouts[far], len(after), far + part, part),
            in_specs=[SMEM] + [LOCAL] * (5 + len(pieces)) + [ANY] * len(after),
            out_specs=[LOCAL] * len(pieces),
            out_shape=shapes(far),
            input_output_aliases={6 + d: d for d in range(len(pieces))},
            scratch_shapes=[extended, extended, pltpu.VMEM((tokens, HD), jnp.float32)],
            compiler_params=params,
            cost_estimate=cost(1, 3 * 2**20),
            name="far_%d" % part,
        )(span_order, own, lse, q, *x, *pieces, *after)

    def across(a, d):
        return lax.ppermute(a, "seq", [(i, i ^ d) for i in range(ring)])

    def start(h, pieces):
        if len(pieces) == ring:
            landed[h] = [(pieces[0], 0, 0)] + [(across(pieces[d], d), 0, d) for d in range(1, ring)]
        elif len(pieces) == 2:
            moving[h] = (pieces[0], across(pieces[1], 2))
        else:
            whole = lax.all_to_all(pieces[0], "seq", split_axis=0, concat_axis=0, tiled=True)
            landed[h] = [(whole, s, None) for s in range(ring)]

    def relay(h, done):
        near_rows, got = moving[h]
        both = pl.pallas_call(
            functools.partial(relay_kernel, 1),
            in_specs=[LOCAL] * 2 + [ANY],
            out_specs=LOCAL,
            out_shape=jax.ShapeDtypeStruct(got.shape, jnp.bfloat16),
            compiler_params=params,
            cost_estimate=cost(0.1, 2**19),
            name="relay_%d" % h,
        )(near_rows, got, done)
        last = across(both, 1)
        landed[h] = [(near_rows, 0, 0), (got, 0, 2), (last, 0, 1), (last, 1, 3)]
        return both

    def place(order, before, after):
        arrays, items = [], []
        for h in order:
            for a, row, d in landed[h]:
                found = [i for i, b in enumerate(arrays) if b is a]
                if not found:
                    arrays.append(a)
                items.append((found[0] if found else len(arrays) - 1, row, d, h))
        extra = list(after) + ([] if before is None else [before])
        return pl.pallas_call(
            functools.partial(place_kernel, len(arrays), items, heads),
            in_specs=[ANY] * (len(arrays) + len(extra)),
            out_specs=ANY,
            out_shape=jax.ShapeDtypeStruct((piece_rows, ring * width), jnp.bfloat16),
            input_output_aliases={} if before is None else {len(arrays) + len(extra) - 1: 0},
            scratch_shapes=[pltpu.SemaphoreType.DMA((len(items),))],
            compiler_params=params,
            cost_estimate=cost(0.1, 2**20),
            name="place_%d" % order[0],
        )(*arrays, *extra)

    def tie(a, b):
        return lax.optimization_barrier((a, b))[0]

    owned, moving, landed, results = {}, {}, {}, {}

    def own(h, done):
        owned[h] = own_call(h, [done] if done is not None else [])
        return owned[h][0]

    pairs = [far] + near
    far_heads, result, done = {}, None, None
    for op in ORDER:
        kind, i = op[0], int(op[1])
        if kind == "o":
            owned[pairs[i]] = own_call(pairs[i], [] if done is None else [done])
            done = owned[pairs[i]][0]
            if i == 0:
                far_pieces = owned[far][2]
        elif kind == "h":
            held = tie(arrived[i], done)
            far_heads[i] = (held, swapped(held, "head"))
        elif kind == "f":
            far_pieces = far_call(i, *owned[far][:2], far_pieces, far_heads[i], [done])
            done = far_pieces[0]
            if i == 1:
                start(far, far_pieces)
        elif kind == "c":
            xq = arrived[i - 1] if i <= lag else results[i - lag]
            follows = pairs[i + lag] if i + lag < len(pairs) else None
            results[i] = done = cross_call(pairs[i], xq, follows, [done])
        elif kind == "x":
            results[i] = swapped(results[i] if results[i] is done else tie(results[i], done), "span")
        elif kind == "m":
            pieces = merge_call(pairs[i], *owned[pairs[i]], results[i], [done])
            start(pairs[i], pieces)
            done = pieces[0]
        elif kind == "r":
            done = relay(pairs[i], done)
        elif kind == "p":
            result = place([pairs[int(j)] for j in op[1:]], result, [done] if done is not result else [])
            done = result
    return result.reshape(1, 1, piece_rows, ring * width)


def solution(mesh):
    def per_device(queries, keys, values, span_order):
        paired = lax.axis_size("span") == 2 and lax.axis_size("head") == 2
        if paired and lax.axis_size("seq") == 4 and queries.shape[3] == 8 * HD:
            return staggered(queries, keys, values, span_order)
        return gathered(queries, keys, values, span_order)

    return jax.shard_map(
        per_device,
        mesh=mesh,
        in_specs=(
            P(("rep", "span"), "head", None, "seq"),
            P(("rep", "span"), "head", None, "seq"),
            P(("rep", "span"), "head", None, "seq"),
            P("rep"),
        ),
        out_specs=P(("rep", "span"), "head", "seq", None),
        check_vma=False,
    )
```

```python
import functools
import math

import jax
import jax.numpy as jnp
from jax import lax
from jax.experimental import pallas as pl
from jax.experimental.pallas import tpu as pltpu
from jax.sharding import PartitionSpec as P

HD = 128
LOG2E = math.log2(math.e)
SCALE2 = LOG2E / math.sqrt(HD)
ROWS = 512
VMEM = 24 * 2**20
ANY = pl.BlockSpec(memory_space=pl.ANY)
SMEM = pl.BlockSpec(memory_space=pltpu.SMEM)
LOCAL = pl.BlockSpec(memory_space=pltpu.VMEM)
HBM = pl.BlockSpec(memory_space=pltpu.HBM)


def lookup(span_order, block_index):
    table = jnp.arange(span_order.shape[0], dtype=jnp.int32)
    return jnp.sum(
        jnp.where(block_index[:, None] == table[None, :], span_order[None, :], 0), axis=1
    )


def initial(query_heads):
    query_count = query_heads.shape[0]
    local_heads = query_heads.shape[1]
    return (
        jnp.full((local_heads, query_count), -1e30, jnp.float32),
        jnp.zeros((local_heads, query_count), jnp.float32),
        jnp.zeros((local_heads, query_count, HD), jnp.float32),
    )


def attend(running, query_heads, key_piece, value_piece, block_span, own_span, bias_rate):
    block_count = key_piece.shape[0]
    piece_rows = key_piece.shape[1]
    local_heads = key_piece.shape[2] // HD
    key_count = block_count * piece_rows
    score_scale = 1.0 / math.sqrt(HD)
    key_spans = jnp.repeat(block_span, piece_rows)
    allowed = key_spans <= own_span
    distance_bias = (own_span - key_spans).astype(jnp.float32) * jnp.float32(bias_rate)
    block_size = 1024
    block_total = key_count // block_size
    key_blocks = key_piece.reshape(block_total, block_size, local_heads, HD)
    value_blocks = value_piece.reshape(block_total, block_size, local_heads, HD)
    allow_blocks = allowed.reshape(block_total, block_size)
    bias_blocks = distance_bias.reshape(block_total, block_size)

    def advance(status, block_item):
        key_block, value_block, allow_block, bias_block = block_item
        maxima, totals, weighted = status
        scores = (
            jnp.einsum("qhd,khd->hqk", query_heads, key_block, preferred_element_type=jnp.float32)
            * score_scale
        )
        scores = scores - bias_block[None, None, :]
        scores = jnp.where(allow_block[None, None, :], scores, jnp.float32(-1e30))
        new_max = jnp.maximum(maxima, jnp.max(scores, axis=2))
        weights = jnp.where(
            allow_block[None, None, :], jnp.exp(scores - new_max[:, :, None]), 0.0
        ).astype(jnp.bfloat16)
        shrink = jnp.exp(maxima - new_max)
        totals = totals * shrink + jnp.sum(weights.astype(jnp.float32), axis=2)
        weighted = weighted * shrink[:, :, None] + jnp.einsum(
            "hqk,khd->hqd", weights, value_block, preferred_element_type=jnp.float32
        )
        return ((new_max, totals, weighted), None)

    running, unused = lax.scan(
        advance, running, (key_blocks, value_blocks, allow_blocks, bias_blocks)
    )
    return running


def finish(running):
    maxima, totals, weighted = running
    local_heads = weighted.shape[0]
    query_count = weighted.shape[1]
    output = (weighted / totals[:, :, None]).transpose(1, 0, 2)
    return output.reshape(1, 1, query_count, local_heads * HD).astype(jnp.bfloat16)


def gathered(queries, keys, values, span_order):
    half_rows = queries.shape[2]
    local_width = queries.shape[3]
    local_heads = local_width // HD
    halves = lax.axis_size("head")
    bias_rate = 1.0 / (2.0 * span_order.shape[0])
    own_span = lookup(span_order, jnp.reshape(lax.axis_index("span"), (1,)))[0]
    query_heads = queries.reshape(half_rows, local_heads, HD)
    pieces = (
        lax.all_gather(keys, ("span", "head"), axis=0, tiled=True),
        lax.all_gather(values, ("span", "head"), axis=0, tiled=True),
    )
    count = pieces[0].shape[0]
    block_index = jnp.arange(count, dtype=jnp.int32) // halves
    key_piece = pieces[0].reshape(count, half_rows, local_width)
    value_piece = pieces[1].reshape(count, half_rows, local_width)
    running = attend(
        initial(query_heads),
        query_heads,
        key_piece,
        value_piece,
        lookup(span_order, block_index),
        own_span,
        bias_rate,
    )
    result = finish(running)
    return lax.all_to_all(result, "seq", split_axis=2, concat_axis=3, tiled=True)


def rows_by_cols(a, b):
    return lax.dot_general(a, b, (((1,), (1,)), ((), ())), preferred_element_type=jnp.float32)


def attend_rows(q, k0, k1, v0, v1):
    parts = []
    for k, v in ((k0, v0), (k1, v1)):
        scores = rows_by_cols(q, k[...])
        top = jnp.max(scores, axis=1, keepdims=True) * SCALE2
        weights = jnp.exp2(scores * SCALE2 - top).astype(jnp.bfloat16)
        parts.append((jnp.dot(weights, v[...], preferred_element_type=jnp.float32), top))
    (a0, m0), (a1, m1) = parts
    top = jnp.maximum(m0, m1)
    both = a0 * jnp.exp2(m0 - top) + a1 * jnp.exp2(m1 - top)
    return both[:, :HD], both[:, HD:], top


def roles(order):
    group = lax.axis_index("span")
    behind = order[group] - order[1 - group]
    bias_rate = LOG2E / (2.0 * order.shape[0])
    return behind > 0, behind.astype(jnp.float32) * jnp.float32(bias_rate)


def load_values(v0, v1, e0, e1):
    e0[:, :HD] = v0
    e1[:, :HD] = v1


def fill_ones(e0, e1):
    for e in (e0, e1):
        e[:, HD:] = jnp.ones_like(e[:, HD:])


def put_pieces(own, out, layout):
    if layout is None:
        out[0][...] = own[...].astype(jnp.bfloat16)
        return
    me = lax.axis_index("seq")
    size = own.shape[0] // sum(len(ds) for ds in layout)
    for array, ds in zip(out, layout):
        for j, d in enumerate(ds):
            start = pl.multiple_of(lax.bitwise_xor(me, d) * size, size)
            array[pl.ds(j * size, size), :] = own[pl.ds(start, size), :].astype(jnp.bfloat16)


def span_of(part, count=1):
    return pl.ds(part * HD, count * HD)


ORDER = (
    "o0", "o1", "h0", "f0", "c1", "x1", "h1", "f1", "c2", "x2", "o2", "m1", "c3", "x3", "r0", "m2", "o3", "r1", "m3", "r2", "p01", "p2", "p3",
)
LAST = ((0,), (1,), (2,), (3,))
RELAYED = 3


def own_kernel(layout, after, head, order, q, k0, k1, v0, v1, *rest):
    own, lse, *out = rest[after:-2]
    e0, e1 = rest[-2:]
    fill_ones(e0, e1)
    for p in range(2):
        cols = span_of(p)
        load_values(v0[:, span_of(head + p)], v1[:, span_of(head + p)], e0, e1)
        for r in range(0, q.shape[0], ROWS):
            rows = pl.ds(r, ROWS)
            o, l, m = attend_rows(
                q[rows, span_of(head + p)], k0.at[:, span_of(head + p)], k1.at[:, span_of(head + p)], e0, e1
            )
            own[rows, cols] = o / l
            lse[rows, cols] = m + jnp.log2(l)
    put_pieces(own, out, layout)


def cross_kernel(after, following, head, order, xq, q, k0, k1, v0, v1, *rest):
    send, e0, e1 = rest[after:]
    tokens = q.shape[0]
    high, unused_shift = roles(order)

    if following is not None:
        @pl.when(high)
        def _():
            send[pl.ds(0, tokens), :] = q[:, span_of(following, 2)]

    @pl.when(jnp.logical_not(high))
    def _():
        fill_ones(e0, e1)
        for p in range(2):
            cols = span_of(p)
            load_values(v0[:, span_of(head + p)], v1[:, span_of(head + p)], e0, e1)
            levels = []
            for r in range(0, tokens, ROWS):
                o, l, m = attend_rows(
                    xq[pl.ds(r, ROWS), cols], k0.at[:, span_of(head + p)], k1.at[:, span_of(head + p)], e0, e1
                )
                send[pl.ds(r, ROWS), cols] = (o / l).astype(jnp.bfloat16)
                level = m + jnp.log2(l)
                levels += [level[c : c + HD, :].T[:1, :] for c in range(0, ROWS, HD)]
            level = jnp.concatenate(levels, axis=0)
            terms = []
            for _ in range(3):
                term = level.astype(jnp.bfloat16).astype(jnp.float32)
                level = level - term
                terms.append(term)
            terms.append(jnp.zeros_like(level))
            send[pl.ds(tokens, 4 * len(levels)), cols] = jnp.concatenate(terms, axis=0).astype(jnp.bfloat16)


def blend(o0, l0, o1, l1):
    top = jnp.maximum(l0, l1)
    w0, w1 = jnp.exp2(l0 - top), jnp.exp2(l1 - top)
    return (o0 * w0 + o1 * w1) / (w0 + w1)


def copy_in(pairs, sems):
    copies = [pltpu.make_async_copy(s, d, sems.at[i]) for i, (s, d) in enumerate(pairs)]
    for c in copies:
        c.start()
    for c in copies:
        c.wait()


def merge_kernel(layout, after, order, own, lse, r, *rest):
    *out, both = rest[(len(layout) if layout else 1) + after :]
    tokens, width = own.shape
    high, shift = roles(order)

    @pl.when(high)
    def _():
        count = tokens // HD
        for c in range(0, width, HD):
            cols = pl.ds(c, HD)
            terms = r[pl.ds(tokens, 4 * count), cols].astype(jnp.float32)
            level = terms[:count] + terms[count : 2 * count] + terms[2 * count : 3 * count]
            for i in range(count):
                rows = pl.ds(i * HD, HD)
                far = jnp.broadcast_to(level[i : i + 1, :], (HD, HD)).T - shift
                both[rows, cols] = blend(own[rows, cols], lse[rows, cols], r[rows, cols].astype(jnp.float32), far)
        put_pieces(both, out, layout)


def far_kernel(layout, after, head, part, order, own, lse, q, x0, x1, *rest):
    *out, e0, e1, both = rest[len(layout) + after :]
    cols = span_of(part)
    high, shift = roles(order)

    @pl.when(high)
    def _():
        fill_ones(e0, e1)
        load_values(x0[:, span_of(1)], x1[:, span_of(1)], e0, e1)
        for i in range(0, own.shape[0], ROWS):
            rows = pl.ds(i, ROWS)
            o, l, m = attend_rows(q[rows, span_of(head)], x0.at[:, span_of(0)], x1.at[:, span_of(0)], e0, e1)
            level = m + jnp.log2(l) - shift
            both[rows, :] = blend(own[rows, cols], lse[rows, cols], o / l, level)
        put_pieces(both, [piece.at[:, cols] for piece in out], layout)


def relay_kernel(after, near, got, *rest):
    out = rest[-1]
    size = out.shape[0] // 2
    out[pl.ds(0, size), :] = near[pl.ds(size, size), :]
    out[pl.ds(size, size), :] = got[pl.ds(size, size), :]


def place_kernel(count, items, total, *rest):
    arrays = rest[:count]
    out, sems = rest[-2:]
    me = lax.axis_index("seq")
    size = out.shape[0]
    pairs = []
    for i, row, d, h in items:
        start = row * total * HD + h * HD if d is None else pl.multiple_of((lax.bitwise_xor(me, d) * total + h) * HD, HD)
        pairs.append((arrays[i].at[pl.ds(row * size, size), :], out.at[:, pl.ds(start, arrays[i].shape[1])]))
    copy_in(pairs, sems)


def first_kernel(far, order, q, k, v, x0, x1, stage, sems):
    high, unused_shift = roles(order)

    @pl.when(high)
    def _():
        copy_in([(q.at[:, span_of(2 * i, 2)], stage.at[i]) for i in range(2)], sems)

    @pl.when(jnp.logical_not(high))
    def _():
        copy_in(
            [
                (a.at[:, span_of(far + i)], stage.at[i, :, span_of(j)])
                for i in range(2) for j, a in enumerate((k, v))
            ],
            sems,
        )

    copy_in([(stage.at[0], x0), (stage.at[1], x1)], sems)


def cost(units, size):
    return pl.CostEstimate(flops=int(units * 3e9), bytes_accessed=size, transcendentals=0)


def staggered(queries, keys, values, span_order):
    q, k, v = queries[0, 0], keys[0, 0], values[0, 0]
    tokens, width = q.shape
    heads = width // HD
    ring = lax.axis_size("seq")
    piece_rows = tokens // ring
    swap = [(0, 1), (1, 0)]
    far = heads - 2
    near = list(range(0, far, 2))
    lag = 2
    layouts = {h: ((0, 1), (2, 3)) if i < RELAYED else LAST for i, h in enumerate([far] + near)}

    params = pltpu.CompilerParams(vmem_limit_bytes=VMEM)
    sent_rows = tokens + 4 * (tokens // HD)
    wide = jax.ShapeDtypeStruct((tokens, 2 * HD), jnp.float32)
    two = jax.ShapeDtypeStruct((tokens, 2 * HD), jnp.bfloat16)
    extended = pltpu.VMEM((tokens, 2 * HD), jnp.bfloat16)

    def swapped(a, axis):
        return lax.ppermute(a, axis, swap)

    k_far, v_far = swapped(k, "head"), swapped(v, "head")
    x0, x1 = pl.pallas_call(
        functools.partial(first_kernel, far),
        in_specs=[SMEM] + [HBM] * 3,
        out_specs=[ANY] * 2,
        out_shape=[two, two],
        scratch_shapes=[pltpu.VMEM((2, tokens, 2 * HD), jnp.bfloat16), pltpu.SemaphoreType.DMA((4,))],
        compiler_params=params,
        cost_estimate=cost(0, 2 * 2**20),
        name="first",
    )(span_order, q, k, v)
    arrived = [swapped(x0, "span"), swapped(x1, "span")]

    def shapes(h):
        if layouts[h] is None:
            return [two]
        return [jax.ShapeDtypeStruct((len(ds) * piece_rows, 2 * HD), jnp.bfloat16) for ds in layouts[h]]

    def own_call(h, after):
        result = pl.pallas_call(
            functools.partial(own_kernel, layouts[h], len(after), h),
            in_specs=[SMEM] + [LOCAL] * 5 + [ANY] * len(after),
            out_specs=[LOCAL] * (2 + len(shapes(h))),
            out_shape=[wide, wide] + shapes(h),
            scratch_shapes=[extended, extended],
            compiler_params=params,
            cost_estimate=cost(2, 3 * 2**20),
            name="own_%d" % h,
        )(span_order, q, k, k_far, v, v_far, *after)
        return result[0], result[1], result[2:]

    def cross_call(h, xq, following, after):
        return pl.pallas_call(
            functools.partial(cross_kernel, len(after), following, h),
            in_specs=[SMEM] + [LOCAL] * 6 + [ANY] * len(after),
            out_specs=LOCAL,
            out_shape=jax.ShapeDtypeStruct((sent_rows, 2 * HD), jnp.bfloat16),
            scratch_shapes=[extended, extended],
            compiler_params=params,
            cost_estimate=cost(2, 3 * 2**20),
            name="cross_%d" % h,
        )(span_order, xq, q, k, k_far, v, v_far, *after)

    def merge_call(h, own, lse, pieces, r, after):
        return pl.pallas_call(
            functools.partial(merge_kernel, layouts[h], len(after)),
            in_specs=[SMEM] + [LOCAL] * (3 + len(pieces)) + [ANY] * len(after),
            out_specs=[LOCAL] * len(pieces),
            out_shape=shapes(h),
            input_output_aliases={4 + d: d for d in range(len(pieces))},
            scratch_shapes=[pltpu.VMEM((tokens, 2 * HD), jnp.float32)],
            compiler_params=params,
            cost_estimate=cost(0.4, 2**20),
            name="merge_%d" % h,
        )(span_order, own, lse, r, *pieces, *after)

    def far_call(part, own, lse, pieces, x, after):
        return pl.pallas_call(
            functools.partial(far_kernel, layouts[far], len(after), far + part, part),
            in_specs=[SMEM] + [LOCAL] * (5 + len(pieces)) + [ANY] * len(after),
            out_specs=[LOCAL] * len(pieces),
            out_shape=shapes(far),
            input_output_aliases={6 + d: d for d in range(len(pieces))},
            scratch_shapes=[extended, extended, pltpu.VMEM((tokens, HD), jnp.float32)],
            compiler_params=params,
            cost_estimate=cost(1, 3 * 2**20),
            name="far_%d" % part,
        )(span_order, own, lse, q, *x, *pieces, *after)

    def across(a, d):
        return lax.ppermute(a, "seq", [(i, i ^ d) for i in range(ring)])

    def start(h, pieces):
        if len(pieces) == ring:
            landed[h] = [(pieces[0], 0, 0)] + [(across(pieces[d], d), 0, d) for d in range(1, ring)]
        elif len(pieces) == 2:
            moving[h] = (pieces[0], across(pieces[1], 2))
        else:
            whole = lax.all_to_all(pieces[0], "seq", split_axis=0, concat_axis=0, tiled=True)
            landed[h] = [(whole, s, None) for s in range(ring)]

    def relay(h, done):
        near_rows, got = moving[h]
        both = pl.pallas_call(
            functools.partial(relay_kernel, 1),
            in_specs=[LOCAL] * 2 + [ANY],
            out_specs=LOCAL,
            out_shape=jax.ShapeDtypeStruct(got.shape, jnp.bfloat16),
            compiler_params=params,
            cost_estimate=cost(0.1, 2**19),
            name="relay_%d" % h,
        )(near_rows, got, done)
        last = across(both, 1)
        landed[h] = [(near_rows, 0, 0), (got, 0, 2), (last, 0, 1), (last, 1, 3)]
        return both

    def place(order, before, after):
        arrays, items = [], []
        for h in order:
            for a, row, d in landed[h]:
                found = [i for i, b in enumerate(arrays) if b is a]
                if not found:
                    arrays.append(a)
                items.append((found[0] if found else len(arrays) - 1, row, d, h))
        extra = list(after) + ([] if before is None else [before])
        return pl.pallas_call(
            functools.partial(place_kernel, len(arrays), items, heads),
            in_specs=[ANY] * (len(arrays) + len(extra)),
            out_specs=ANY,
            out_shape=jax.ShapeDtypeStruct((piece_rows, ring * width), jnp.bfloat16),
            input_output_aliases={} if before is None else {len(arrays) + len(extra) - 1: 0},
            scratch_shapes=[pltpu.SemaphoreType.DMA((len(items),))],
            compiler_params=params,
            cost_estimate=cost(0.1, 2**20),
            name="place_%d" % order[0],
        )(*arrays, *extra)

    def tie(a, b):
        return lax.optimization_barrier((a, b))[0]

    owned, moving, landed, results = {}, {}, {}, {}

    def own(h, done):
        owned[h] = own_call(h, [done] if done is not None else [])
        return owned[h][0]

    pairs = [far] + near
    far_heads, result, done = {}, None, None
    for op in ORDER:
        kind, i = op[0], int(op[1])
        if kind == "o":
            owned[pairs[i]] = own_call(pairs[i], [] if done is None else [done])
            done = owned[pairs[i]][0]
            if i == 0:
                far_pieces = owned[far][2]
        elif kind == "h":
            held = tie(arrived[i], done)
            far_heads[i] = (held, swapped(held, "head"))
        elif kind == "f":
            far_pieces = far_call(i, *owned[far][:2], far_pieces, far_heads[i], [done])
            done = far_pieces[0]
            if i == 1:
                start(far, far_pieces)
        elif kind == "c":
            xq = arrived[i - 1] if i <= lag else results[i - lag]
            follows = pairs[i + lag] if i + lag < len(pairs) else None
            results[i] = done = cross_call(pairs[i], xq, follows, [done])
        elif kind == "x":
            results[i] = swapped(results[i] if results[i] is done else tie(results[i], done), "span")
        elif kind == "m":
            pieces = merge_call(pairs[i], *owned[pairs[i]], results[i], [done])
            start(pairs[i], pieces)
            done = pieces[0]
        elif kind == "r":
            done = relay(pairs[i], done)
        elif kind == "p":
            result = place([pairs[int(j)] for j in op[1:]], result, [done] if done is not result else [])
            done = result
    return result.reshape(1, 1, piece_rows, ring * width)


def solution(mesh):
    def per_device(queries, keys, values, span_order):
        paired = lax.axis_size("span") == 2 and lax.axis_size("head") == 2
        if paired and lax.axis_size("seq") == 4 and queries.shape[3] == 8 * HD:
            return staggered(queries, keys, values, span_order)
        return gathered(queries, keys, values, span_order)

    return jax.shard_map(
        per_device,
        mesh=mesh,
        in_specs=(
            P(("rep", "span"), "head", None, "seq"),
            P(("rep", "span"), "head", None, "seq"),
            P(("rep", "span"), "head", None, "seq"),
            P("rep"),
        ),
        out_specs=P(("rep", "span"), "head", "seq", None),
        check_vma=False,
    )
```
